512 devices in a mesh: row: 64 (over y, x, core), col: 8 (over z).
Axes of the slice: x: 4, y: 8, z: 8, core: 2. Of those that a mesh axis runs over, the one named last changes fastest.
Arguments:
- hidden_states: bfloat16 [16384, 8192], P('row', 'col'), may hold values from -80 to 80, as said below
- sketch_matrix: bfloat16 [8192, 512], P('col'), may hold values from -0.0625 to 0.0625
Outputs:
- q_left: float32 [16384, 512], P(('row', 'col'))
- q_right: float32 [8, 1024, 512], P('col', 'row')
- triangle: float32 [512, 512], replicated
The draws below stay inside these ranges and needn't reach their ends.
Inputs may be any that keep to these rules, and one draw needn't show every extreme that they name: `hidden_states`: real-valued activation rows.
All inputs are finite; a program needn't handle non-finite values.
Results may differ from the reference program's by a relative error of at most 0.0023.
Values may be sent and summed in bfloat16 or wider, within the bound.
No kernel may reach another device: no remote copies, remote signals or barrier semaphores. Data moves between devices by JAX's collectives and lax.ppermute only.
A program may use at most 64 MiB of HBM per device.

```python
import math
import jax
import jax.numpy as jnp
from jax import lax

N = 8192
K = 512
M = 16384
N_COL = 8


def draw_hidden_states(key, part):
    key = jax.random.fold_in(key, 11)
    first, second, third = jax.random.split(key, 3)
    row_scale = jnp.exp(jax.random.uniform(second, (M, 1), jnp.float32, 0.0, math.log(10.0)))
    col_scale = jnp.exp(jax.random.uniform(third, (1, N), jnp.float32, 0.0, math.log(10.0)))
    position = jnp.arange(M, dtype=jnp.float32).reshape(M, 1) / M
    base = jax.random.truncated_normal(first, -4.0, 4.0, (M, N), jnp.float32)
    trend = jnp.exp(math.log(3.0) * position)
    values = 0.05 * row_scale * trend * base * col_scale
    return values.astype(jnp.bfloat16)


def block_levels(rng, shape, pieces, low, largest):
    loudness, own = 1.0, jax.random.fold_in(rng, 6)
    for dim, blocks in pieces:
        steps = jnp.exp(jax.random.uniform(jax.random.fold_in(own, dim), (blocks,), jnp.float32, low / len(pieces), largest / len(pieces)))
        loudness = loudness * jnp.repeat(steps, shape[dim] // blocks).reshape([-1 if axis == dim else 1 for axis in range(len(shape))])
    return loudness


def noise(key, shape, scale, reach, shards=(), kind=jnp.bfloat16):
    level = block_levels(key, shape, shards, -0.22, 0.18) if shards else 1.0
    values = jax.random.normal(key, shape, jnp.float32) * scale * level
    return jnp.minimum(jnp.maximum(values, -reach), reach).astype(kind)


def setup_inputs(seed: int = 0) -> dict:
    key_of = jax.random.split(jax.random.key(seed), 3)
    hidden_states = draw_hidden_states(jax.random.fold_in(key_of[2], 71), 0)
    sketch_matrix = noise(key_of[1], (N, K), N ** -0.5, 0.0625, ((0, 8),))
    return dict(hidden_states=hidden_states, sketch_matrix=sketch_matrix)


def orthonormal(tall):
    gram = jnp.dot(tall.T.astype(jnp.float32), tall.astype(jnp.float32), precision=lax.Precision.HIGHEST, preferred_element_type=jnp.float32)
    lower = jnp.linalg.cholesky(gram)
    basis = jax.scipy.linalg.solve_triangular(lower, tall.T, lower=True).T
    return (basis, lower)

def reference(hidden_states, sketch_matrix):
    sketch = jnp.dot(hidden_states.astype(jnp.float32), sketch_matrix.astype(jnp.float32), preferred_element_type=jnp.float32)
    basis, low_left = orthonormal(sketch)
    basis_half = basis.astype(jnp.bfloat16)
    image = lax.dot_general(hidden_states.astype(jnp.float32), basis_half.astype(jnp.float32), (((0,), (0,)), ((), ())), preferred_element_type=jnp.float32)
    right_basis, low_right = orthonormal(image)
    q_left = basis * math.sqrt(M)
    q_right = (right_basis * math.sqrt(N)).reshape(N_COL, N // N_COL, K)
    triangle = low_right / math.sqrt(N)
    return (q_left, q_right, triangle)
```

```python
import functools
import math

import jax
import jax.numpy as jnp
from jax import lax
from jax.experimental import pallas as pl
from jax.experimental.pallas import tpu as pltpu
from jax.sharding import Mesh
from jax.sharding import PartitionSpec as P

HIGHEST = lax.Precision.HIGHEST
BLOCK = 128
RANK = 8
ROW = ("y", "x", "core")


def across_lanes(piece, column):
    return jnp.broadcast_to(piece[:, column : column + 1], piece.shape)


def across_rows(piece, row):
    return jnp.broadcast_to(piece[row : row + 1, :], piece.shape)


def inverse_factor(block):
    groups = BLOCK // 8
    row = lax.broadcasted_iota(jnp.int32, (8, BLOCK), 0)
    lane = lax.broadcasted_iota(jnp.int32, (8, BLOCK), 1)
    left = [block[8 * i : 8 * i + 8, :] for i in range(groups)]
    right = [jnp.where(lane == row + 8 * i, 1.0, 0.0) for i in range(groups)]
    finished = [jnp.zeros((8, BLOCK), jnp.float32) for _ in range(groups)]
    for first in range(0, BLOCK, RANK):
        group, offset = divmod(first, 8)
        columns = [across_lanes(left[group], first + t) for t in range(RANK)]
        pivot = [[across_rows(columns[u], offset + t) for u in range(t + 1)] for t in range(RANK)]
        on_left = [across_rows(left[group], offset + t) for t in range(RANK)]
        on_right = [across_rows(right[group], offset + t) for t in range(RANK)]
        lower = [[None] * RANK for _ in range(RANK)]
        inverse = [None] * RANK
        for t in range(RANK):
            inverse[t] = 1.0 / pivot[t][t]
            for i in range(t + 1, RANK):
                lower[i][t] = pivot[i][t] * inverse[t]
            for i in range(t + 1, RANK):
                for j in range(t + 1, i + 1):
                    pivot[i][j] = pivot[i][j] - lower[i][t] * pivot[j][t]
                on_left[i] = on_left[i] - lower[i][t] * on_left[t]
                on_right[i] = on_right[i] - lower[i][t] * on_right[t]
        back_left, back_right = [None] * RANK, [None] * RANK
        for t in reversed(range(RANK)):
            back_left[t] = on_left[t] * inverse[t]
            back_right[t] = on_right[t] * inverse[t]
            for s in range(t + 1, RANK):
                back_left[t] = back_left[t] - lower[s][t] * back_left[s]
                back_right[t] = back_right[t] - lower[s][t] * back_right[s]
        for i in range(group, groups):
            if i == group and offset + RANK == 8:
                continue
            change_left = change_right = 0.0
            for t in range(RANK):
                if i == group:
                    factor = jnp.where(row >= offset + RANK, columns[t], 0.0)
                else:
                    factor = across_lanes(left[i], first + t)
                change_left = change_left + factor * back_left[t]
                change_right = change_right + factor * back_right[t]
            left[i] = left[i] - change_left
            right[i] = right[i] - change_right
        for t in range(RANK):
            scaled = on_right[t] * lax.rsqrt(pivot[t][t])
            finished[group] = jnp.where(row == offset + t, scaled, finished[group])
    return jnp.concatenate(finished, axis=0)


def factor_kernel(scale, gram_ref, tall_ref, solved_ref, lower_ref, work, factor):
    size = gram_ref.shape[0]
    work[:size, :] = gram_ref[...]
    work[size:, :] = tall_ref[...]

    def step(index, carry):
        columns = pl.ds(pl.multiple_of(index * BLOCK, BLOCK), BLOCK)
        inverse = inverse_factor(work[columns, columns])
        panel = lax.dot_general(
            work[:, columns],
            inverse,
            (((1,), (1,)), ((), ())),
            precision=HIGHEST,
            preferred_element_type=jnp.float32,
        )
        factor[:, columns] = panel

        @pl.when(index < size // BLOCK - 1)
        def _():
            work[...] -= lax.dot_general(
                panel,
                panel[:size],
                (((1,), (1,)), ((), ())),
                precision=HIGHEST,
                preferred_element_type=jnp.float32,
            )

        return carry

    lax.fori_loop(0, size // BLOCK, step, 0)
    solved_ref[...] = factor[size:, :]
    if lower_ref is not None:
        row = lax.broadcasted_iota(jnp.int32, (size, size), 0)
        column = lax.broadcasted_iota(jnp.int32, (size, size), 1)
        lower_ref[...] = jnp.where(row >= column, factor[:size, :] * scale, 0.0)


def factor_and_solve(gram, tall, scale=None):
    size, rows = gram.shape[0], tall.shape[0]
    shapes = [jax.ShapeDtypeStruct((rows, size), jnp.float32)]
    if scale is None:

        def body(gram_ref, tall_ref, solved_ref, work, factor):
            factor_kernel(None, gram_ref, tall_ref, solved_ref, None, work, factor)

    else:
        shapes.append(jax.ShapeDtypeStruct((size, size), jnp.float32))
        body = functools.partial(factor_kernel, scale)
    held = pltpu.VMEM((size + rows, size), jnp.float32)
    return pl.pallas_call(
        body,
        out_shape=shapes,
        in_specs=[pl.BlockSpec(memory_space=pltpu.VMEM)] * 2,
        out_specs=[pl.BlockSpec(memory_space=pltpu.VMEM)] * len(shapes),
        scratch_shapes=[held, held],
        compiler_params=pltpu.CompilerParams(vmem_limit_bytes=24 * 2**20),
        cost_estimate=pl.CostEstimate(
            flops=2 * size**3, bytes_accessed=8 * size * size, transcendentals=size
        ),
    )(gram, tall)


def gather(piece, axes):
    copies = jnp.broadcast_to(piece[None], (lax.axis_size(axes),) + piece.shape)
    return lax.all_to_all(copies, axes, 0, 0, tiled=True)


def gram_rows(left, right):
    return lax.dot_general(
        left,
        right,
        (((0,), (0,)), ((), ())),
        precision=HIGHEST,
        preferred_element_type=jnp.float32,
    )


def gather_gram(piece):
    size = piece.size
    eight = gather(piece, ("y", "col")).reshape(-1, size)
    four = gather(eight, ("x",)).reshape(-1, size)
    return gather(four, ("core",)).reshape(size, size)


def per_device(hidden_states, sketch_matrix):
    rows, block_width = hidden_states.shape
    size = sketch_matrix.shape[1]
    cols, spread = lax.axis_size("col"), lax.axis_size(ROW)
    total_rows, total_width = rows * spread, block_width * cols
    col = lax.axis_index("col")

    partial_sketch = jnp.dot(hidden_states, sketch_matrix, preferred_element_type=jnp.float32)
    parts = partial_sketch.reshape(cols, rows // cols, size)
    own = jnp.sum(lax.all_to_all(parts, "col", 0, 0, tiled=True), axis=0)
    sketch = gather(own, "col").reshape(rows, size)

    gram = gram_rows(sketch, sketch).reshape(size // cols, cols, size)
    share = lax.dynamic_index_in_dim(gram, col, 1, keepdims=False)
    share = lax.all_to_all(
        share.reshape(spread, 4, size // 4), ("core", "x", "y"), 0, 0, tiled=True
    )
    gram_left = gather_gram(jnp.sum(share, axis=0))
    (basis,) = factor_and_solve(gram_left, sketch)
    q_left = lax.dynamic_slice_in_dim(basis, col * (rows // cols), rows // cols, 0)
    q_left = q_left * math.sqrt(total_rows)

    image_rows = block_width // spread
    partial_image = lax.dot_general(
        hidden_states,
        basis.astype(jnp.bfloat16),
        (((0,), (0,)), ((), ())),
        preferred_element_type=jnp.float32,
    ).reshape(spread // 2, 2, image_rows, size)
    halves = jnp.sum(lax.all_to_all(partial_image, "core", 1, 1, tiled=True), axis=1)
    parts = lax.all_to_all(halves.astype(jnp.bfloat16), ("y", "x"), 0, 0, tiled=True)
    image = jnp.sum(parts.astype(jnp.float32), axis=0)

    near = gather(image, ("x", "core")).reshape(-1, size)
    start = (lax.axis_index("core") * 4 + lax.axis_index("x")) * (size // 8)
    chosen = lax.dynamic_slice_in_dim(near, start, size // 8, 1)
    share = gram_rows(chosen, near).reshape(size // 8, 4, size // 4)
    share = lax.all_to_all(share, ("y", "col"), 0, 0, tiled=True)
    gram_right = gather_gram(jnp.sum(share, axis=0))
    right, triangle = factor_and_solve(gram_right, image, 1.0 / math.sqrt(total_width))
    q_right = (right * math.sqrt(total_width)).reshape(1, image_rows, size)
    return (q_left, q_right, triangle)


def solution(mesh):
    fine = Mesh(mesh.devices.reshape(8, 4, 2, 8), ROW + ("col",))
    return jax.shard_map(
        per_device,
        mesh=fine,
        in_specs=(P(ROW, "col"), P("col", None)),
        out_specs=(P(ROW + ("col",), None), P("col", ROW, None), P()),
        check_vma=False,
    )
```

```python
import functools
import math

import jax
import jax.numpy as jnp
from jax import lax
from jax.experimental import pallas as pl
from jax.experimental.pallas import tpu as pltpu
from jax.sharding import Mesh
from jax.sharding import PartitionSpec as P

HIGHEST = lax.Precision.HIGHEST
BLOCK = 128
RANK = 8
ROW = ("y", "x", "core")


def across_lanes(piece, column):
    place = jnp.full(piece.shape, column, jnp.int32)
    return jnp.take_along_axis(piece, place, axis=1, mode="promise_in_bounds")


def across_rows(piece, row):
    return jnp.broadcast_to(piece[row : row + 1, :], piece.shape)


def inverse_factor(block):
    groups = BLOCK // 8
    row = lax.broadcasted_iota(jnp.int32, (8, BLOCK), 0)
    lane = lax.broadcasted_iota(jnp.int32, (8, BLOCK), 1)
    left = [block[8 * i : 8 * i + 8, :] for i in range(groups)]
    right = [jnp.where(lane == row + 8 * i, 1.0, 0.0) for i in range(groups)]
    finished = [jnp.zeros((8, BLOCK), jnp.float32) for _ in range(groups)]
    for first in range(0, BLOCK, RANK):
        group, offset = divmod(first, 8)
        columns = [across_lanes(left[group], first + t) for t in range(RANK)]
        pivot = [[across_rows(columns[u], offset + t) for u in range(t + 1)] for t in range(RANK)]
        on_left = [across_rows(left[group], offset + t) for t in range(RANK)]
        on_right = [across_rows(right[group], offset + t) for t in range(RANK)]
        lower = [[None] * RANK for _ in range(RANK)]
        inverse = [None] * RANK
        for t in range(RANK):
            inverse[t] = 1.0 / pivot[t][t]
            for i in range(t + 1, RANK):
                lower[i][t] = pivot[i][t] * inverse[t]
            for i in range(t + 1, RANK):
                for j in range(t + 1, i + 1):
                    pivot[i][j] = pivot[i][j] - lower[i][t] * pivot[j][t]
                on_left[i] = on_left[i] - lower[i][t] * on_left[t]
                on_right[i] = on_right[i] - lower[i][t] * on_right[t]
        back_left, back_right = [None] * RANK, [None] * RANK
        for t in reversed(range(RANK)):
            back_left[t] = on_left[t] * inverse[t]
            back_right[t] = on_right[t] * inverse[t]
            for s in reversed(range(t + 1, RANK)):
                back_left[t] = back_left[t] - lower[s][t] * back_left[s]
                back_right[t] = back_right[t] - lower[s][t] * back_right[s]
        for i in range(group, groups):
            if i == group and offset + RANK == 8:
                continue
            new_left, new_right = left[i], right[i]
            for t in reversed(range(RANK)):
                if i == group:
                    factor = jnp.where(row >= offset + RANK, columns[t], 0.0)
                else:
                    factor = across_lanes(left[i], first + t)
                new_left = new_left - factor * back_left[t]
                new_right = new_right - factor * back_right[t]
            left[i], right[i] = new_left, new_right
        for t in range(RANK):
            scaled = on_right[t] * lax.rsqrt(pivot[t][t])
            finished[group] = jnp.where(row == offset + t, scaled, finished[group])
    return jnp.concatenate(finished, axis=0)


def times_transposed(left, right):
    return lax.dot_general(
        left,
        right,
        (((1,), (1,)), ((), ())),
        precision=HIGHEST,
        preferred_element_type=jnp.float32,
    )


def factor_blocks(gram_ref, tall_ref, work, factor, inverse):
    size = gram_ref.shape[0]
    work[:size, :] = gram_ref[...]
    work[size:, :] = tall_ref[...]

    def step(index, carry):
        here = pl.ds(pl.multiple_of(index * BLOCK, BLOCK), BLOCK)
        inverse[...] = inverse_factor(work[here, here])
        for block in range(size // BLOCK):
            first, after = block * BLOCK, (block + 1) * BLOCK

            @pl.when(index == block)
            def _(first=first, after=after):
                panel = times_transposed(work[first:, first:after], inverse[...])
                factor[first:, first:after] = panel
                if after < size:
                    below, right = panel[BLOCK:], panel[BLOCK : size - first]
                    work[after:, after:] -= times_transposed(below, right)

        return carry

    lax.fori_loop(0, size // BLOCK, step, 0)


def left_kernel(gram_ref, tall_ref, turned_ref, solved_ref, image_ref, work, factor, inverse):
    size = gram_ref.shape[0]
    factor_blocks(gram_ref, tall_ref, work, factor, inverse)
    basis = factor[size:, :]
    solved_ref[...] = basis
    image = jnp.dot(
        turned_ref[...], basis.astype(jnp.bfloat16), preferred_element_type=jnp.float32
    )
    halves, rows, _ = image_ref.shape
    image = image.reshape(rows // 16, halves, 16, size)
    for half in range(halves):
        image_ref[half] = image[:, half].reshape(rows, size)


def right_kernel(scales, gram_ref, tall_ref, solved_ref, lower_ref, work, factor, inverse):
    size = gram_ref.shape[0]
    factor_blocks(gram_ref, tall_ref, work, factor, inverse)
    solved_ref[...] = factor[size:, :] * scales[0]
    row = lax.broadcasted_iota(jnp.int32, (size, size), 0)
    column = lax.broadcasted_iota(jnp.int32, (size, size), 1)
    lower_ref[...] = jnp.where(row >= column, factor[:size, :] * scales[1], 0.0)


def call_factor(kernel, shapes, operands):
    size, rows = operands[0].shape[0], operands[1].shape[0]
    held = pltpu.VMEM((size + rows, size), jnp.float32)
    return pl.pallas_call(
        kernel,
        out_shape=[jax.ShapeDtypeStruct(shape, jnp.float32) for shape in shapes],
        in_specs=[pl.BlockSpec(memory_space=pltpu.VMEM)] * len(operands),
        out_specs=[pl.BlockSpec(memory_space=pltpu.VMEM)] * len(shapes),
        scratch_shapes=[held, held, pltpu.VMEM((BLOCK, BLOCK), jnp.float32)],
        compiler_params=pltpu.CompilerParams(vmem_limit_bytes=32 * 2**20),
        cost_estimate=pl.CostEstimate(
            flops=2 * size**3, bytes_accessed=8 * size * size, transcendentals=size
        ),
    )(*operands)


def gather(piece, axes):
    copies = jnp.broadcast_to(piece[None], (lax.axis_size(axes),) + piece.shape)
    return lax.all_to_all(copies, axes, 0, 0, tiled=True)


def gram_rows(left, right):
    return lax.dot_general(
        left,
        right,
        (((0,), (0,)), ((), ())),
        precision=HIGHEST,
        preferred_element_type=jnp.float32,
    )


def gather_gram(piece):
    size = piece.size
    eight = gather(piece, ("y", "col")).reshape(-1, size)
    four = gather(eight, ("x",)).reshape(-1, size)
    return gather(four, ("core",)).reshape(size, size)


def per_device(hidden_states, sketch_matrix):
    rows, block_width = hidden_states.shape
    size = sketch_matrix.shape[1]
    cols, spread = lax.axis_size("col"), lax.axis_size(ROW)
    total_rows, total_width = rows * spread, block_width * cols
    col = lax.axis_index("col")

    partial_sketch = jnp.dot(hidden_states, sketch_matrix, preferred_element_type=jnp.float32)
    parts = partial_sketch.reshape(cols, rows // cols, size)
    own = jnp.sum(lax.all_to_all(parts, "col", 0, 0, tiled=True), axis=0)
    sketch = gather(own, "col").reshape(rows, size)

    gram = gram_rows(sketch, sketch).reshape(size // cols, cols, size)
    share = lax.dynamic_index_in_dim(gram, col, 1, keepdims=False)
    share = lax.all_to_all(
        share.reshape(spread, 4, size // 4), ("core", "x", "y"), 0, 0, tiled=True
    )
    gram_left = gather_gram(jnp.sum(share, axis=0))
    image_rows = block_width // spread
    basis, partial_image = call_factor(
        left_kernel,
        [(rows, size), (2, block_width // 2, size)],
        [gram_left, sketch, hidden_states.T],
    )
    q_left = lax.dynamic_slice_in_dim(basis, col * (rows // cols), rows // cols, 0)
    q_left = q_left * math.sqrt(total_rows)

    halves = jnp.sum(lax.all_to_all(partial_image, "core", 0, 0, tiled=True), axis=0)
    parts = halves.astype(jnp.bfloat16).reshape(spread // 2, image_rows, size)
    parts = lax.all_to_all(parts, ("y", "x"), 0, 0, tiled=True)
    image = jnp.sum(parts.astype(jnp.float32), axis=0)

    near = gather(image, ("x", "core")).reshape(-1, size)
    start = (lax.axis_index("core") * 4 + lax.axis_index("x")) * (size // 8)
    chosen = lax.dynamic_slice_in_dim(near, start, size // 8, 1)
    share = gram_rows(chosen, near).reshape(size // 8, 4, size // 4)
    share = lax.all_to_all(share, ("y", "col"), 0, 0, tiled=True)
    gram_right = gather_gram(jnp.sum(share, axis=0))
    scales = (math.sqrt(total_width), 1.0 / math.sqrt(total_width))
    q_right, triangle = call_factor(
        functools.partial(right_kernel, scales),
        [(image_rows, size), (size, size)],
        [gram_right, image],
    )
    return (q_left, q_right.reshape(1, image_rows, size), triangle)


def solution(mesh):
    fine = Mesh(mesh.devices.reshape(8, 4, 2, 8), ROW + ("col",))
    return jax.shard_map(
        per_device,
        mesh=fine,
        in_specs=(P(ROW, "col"), P("col", None)),
        out_specs=(P(ROW + ("col",), None), P("col", ROW, None), P()),
        check_vma=False,
    )
```

```python
import functools
import math

import jax
import jax.numpy as jnp
from jax import lax
from jax.experimental import pallas as pl
from jax.experimental.pallas import tpu as pltpu
from jax.sharding import Mesh
from jax.sharding import PartitionSpec as P

HIGHEST = lax.Precision.HIGHEST
BLOCK = 128
RANK = 8
ROW = ("y", "x", "core")


def across_lanes(piece, column):
    place = jnp.full(piece.shape, column, jnp.int32)
    return jnp.take_along_axis(piece, place, axis=1, mode="promise_in_bounds")


def across_rows(piece, row):
    return jnp.broadcast_to(piece[row : row + 1, :], piece.shape)


def inverse_factor(block):
    groups = BLOCK // 8
    row = lax.broadcasted_iota(jnp.int32, (8, BLOCK), 0)
    lane = lax.broadcasted_iota(jnp.int32, (8, BLOCK), 1)
    left = [block[8 * i : 8 * i + 8, :] for i in range(groups)]
    right = [jnp.where(lane == row + 8 * i, 1.0, 0.0) for i in range(groups)]
    finished = [jnp.zeros((8, BLOCK), jnp.float32) for _ in range(groups)]
    for first in range(0, BLOCK, RANK):
        group, offset = divmod(first, 8)
        columns = [across_lanes(left[group], first + t) for t in range(RANK)]
        pivot = [[across_rows(columns[u], offset + t) for u in range(t + 1)] for t in range(RANK)]
        on_left = [across_rows(left[group], offset + t) for t in range(RANK)]
        on_right = [across_rows(right[group], offset + t) for t in range(RANK)]
        lower = [[None] * RANK for _ in range(RANK)]
        inverse = [None] * RANK
        for t in range(RANK):
            inverse[t] = 1.0 / pivot[t][t]
            for i in range(t + 1, RANK):
                lower[i][t] = pivot[i][t] * inverse[t]
            for i in range(t + 1, RANK):
                for j in range(t + 1, i + 1):
                    pivot[i][j] = pivot[i][j] - lower[i][t] * pivot[j][t]
                on_left[i] = on_left[i] - lower[i][t] * on_left[t]
                on_right[i] = on_right[i] - lower[i][t] * on_right[t]
        back_left, back_right = [None] * RANK, [None] * RANK
        for t in reversed(range(RANK)):
            back_left[t] = on_left[t] * inverse[t]
            back_right[t] = on_right[t] * inverse[t]
            for s in reversed(range(t + 1, RANK)):
                back_left[t] = back_left[t] - lower[s][t] * back_left[s]
                back_right[t] = back_right[t] - lower[s][t] * back_right[s]
        for i in range(group, groups):
            if i == group and offset + RANK == 8:
                continue
            new_left, new_right = left[i], right[i]
            for t in reversed(range(RANK)):
                if i == group:
                    factor = jnp.where(row >= offset + RANK, columns[t], 0.0)
                else:
                    factor = across_lanes(left[i], first + t)
                new_left = new_left - factor * back_left[t]
                new_right = new_right - factor * back_right[t]
            left[i], right[i] = new_left, new_right
        for t in range(RANK):
            scaled = on_right[t] * lax.rsqrt(pivot[t][t])
            finished[group] = jnp.where(row == offset + t, scaled, finished[group])
    return jnp.concatenate(finished, axis=0)


def times_transposed(left, right):
    return lax.dot_general(
        left,
        right,
        (((1,), (1,)), ((), ())),
        precision=HIGHEST,
        preferred_element_type=jnp.float32,
    )


def factor_blocks(gram_ref, tall_ref, work, factor, inverse):
    size = gram_ref.shape[0]
    work[size:, :] = tall_ref[...]

    def step(index, carry):
        here = pl.ds(pl.multiple_of(index * BLOCK, BLOCK), BLOCK)
        inverse[...] = inverse_factor(work[here, here])
        for block in range(size // BLOCK):
            first, after = block * BLOCK, (block + 1) * BLOCK

            @pl.when(index == block)
            def _(first=first, after=after):
                panel = times_transposed(work[first:, first:after], inverse[...])
                factor[first:, first:after] = panel
                if after < size:
                    below, right = panel[BLOCK:], panel[BLOCK : size - first]
                    work[after:, after:] -= times_transposed(below, right)

        return carry

    lax.fori_loop(0, size // BLOCK, step, 0)


def left_kernel(gram_ref, tall_ref, turned_ref, solved_ref, image_ref, work, factor, inverse):
    size = gram_ref.shape[0]
    for place in range(size // 8):
        y, x, core = place // 8, place // 2 % 4, place % 2
        came = (core * 4 + x) * 8 + y
        work[8 * place : 8 * place + 8, :] = gram_ref[8 * came : 8 * came + 8, :]
    factor_blocks(gram_ref, tall_ref, work, factor, inverse)
    basis = factor[size:, :]
    solved_ref[...] = basis
    image = jnp.dot(
        turned_ref[...], basis.astype(jnp.bfloat16), preferred_element_type=jnp.float32
    )
    halves, rows, _ = image_ref.shape
    image = image.reshape(rows // 16, halves, 16, size)
    for half in range(halves):
        image_ref[half] = image[:, half].reshape(rows, size)


def right_kernel(scales, gram_ref, tall_ref, solved_ref, lower_ref, work, factor, inverse):
    size = gram_ref.shape[0]
    work[:size, :] = gram_ref[...]
    factor_blocks(gram_ref, tall_ref, work, factor, inverse)
    solved_ref[...] = factor[size:, :] * scales[0]
    row = lax.broadcasted_iota(jnp.int32, (size, size), 0)
    column = lax.broadcasted_iota(jnp.int32, (size, size), 1)
    lower_ref[...] = jnp.where(row >= column, factor[:size, :] * scales[1], 0.0)


def call_factor(kernel, shapes, operands):
    size, rows = operands[0].shape[0], operands[1].shape[0]
    held = pltpu.VMEM((size + rows, size), jnp.float32)
    return pl.pallas_call(
        kernel,
        out_shape=[jax.ShapeDtypeStruct(shape, jnp.float32) for shape in shapes],
        in_specs=[pl.BlockSpec(memory_space=pltpu.VMEM)] * len(operands),
        out_specs=[pl.BlockSpec(memory_space=pltpu.VMEM)] * len(shapes),
        scratch_shapes=[held, held, pltpu.VMEM((BLOCK, BLOCK), jnp.float32)],
        compiler_params=pltpu.CompilerParams(vmem_limit_bytes=32 * 2**20),
        cost_estimate=pl.CostEstimate(
            flops=2 * size**3, bytes_accessed=8 * size * size, transcendentals=size
        ),
    )(*operands)


def gather(piece, axes):
    copies = jnp.broadcast_to(piece[None], (lax.axis_size(axes),) + piece.shape)
    return lax.all_to_all(copies, axes, 0, 0, tiled=True)


def pack(values):
    power = jnp.clip(jnp.ceil(jnp.log2(jnp.max(jnp.abs(values)))), -100.0, 100.0)
    scaled = (values * jnp.exp2(14.0 - power)).astype(jnp.float16)
    lanes = jnp.full((*values.shape[:-1], 128), power, jnp.float16)
    return jnp.concatenate([scaled, lanes], axis=-1)


def unpack(message):
    size = message.shape[-1] - 128
    power = message[..., size : size + 1].astype(jnp.float32)
    return message[..., :size].astype(jnp.float32) * jnp.exp2(power - 14.0)


def gram_rows(left, right):
    return lax.dot_general(
        left,
        right,
        (((0,), (0,)), ((), ())),
        precision=HIGHEST,
        preferred_element_type=jnp.float32,
    )


def gather_gram(piece):
    size = piece.size
    eight = gather(piece, ("y", "col")).reshape(-1, size)
    four = gather(eight, ("x",)).reshape(-1, size)
    return gather(four, ("core",)).reshape(size, size)


def per_device(hidden_states, sketch_matrix):
    rows, block_width = hidden_states.shape
    size = sketch_matrix.shape[1]
    cols, spread = lax.axis_size("col"), lax.axis_size(ROW)
    total_rows, total_width = rows * spread, block_width * cols
    col = lax.axis_index("col")

    partial_sketch = jnp.dot(hidden_states, sketch_matrix, preferred_element_type=jnp.float32)
    parts = pack(partial_sketch).reshape(cols, rows // cols, size + 128)
    own = jnp.sum(unpack(lax.all_to_all(parts, "col", 0, 0, tiled=True)), axis=0)
    sketch = unpack(gather(pack(own), "col")).reshape(rows, size)

    gram = gram_rows(sketch, sketch).reshape(size // cols, cols, size)
    share = lax.dynamic_index_in_dim(gram, col, 1, keepdims=False)
    share = lax.all_to_all(share.reshape(spread, 4, size // 4), ROW, 0, 0, tiled=True)
    gram_left = gather_gram(jnp.sum(share, axis=0))
    image_rows = block_width // spread
    basis, partial_image = call_factor(
        left_kernel,
        [(rows, size), (2, block_width // 2, size)],
        [gram_left, sketch, hidden_states.T],
    )
    q_left = lax.dynamic_slice_in_dim(basis, col * (rows // cols), rows // cols, 0)
    q_left = q_left * math.sqrt(total_rows)

    halves = jnp.sum(lax.all_to_all(partial_image, "core", 0, 0, tiled=True), axis=0)
    parts = halves.astype(jnp.bfloat16).reshape(spread // 2, image_rows, size)
    parts = lax.all_to_all(parts, ("y", "x"), 0, 0, tiled=True)
    image = jnp.sum(parts.astype(jnp.float32), axis=0)

    near = gather(image, ("x", "core")).reshape(-1, size)
    start = (lax.axis_index("core") * 4 + lax.axis_index("x")) * (size // 8)
    chosen = lax.dynamic_slice_in_dim(near, start, size // 8, 1)
    share = gram_rows(chosen, near).reshape(size // 8, 4, size // 4)
    share = lax.all_to_all(share, ("y", "col"), 0, 0, tiled=True)
    gram_right = gather_gram(jnp.sum(share, axis=0))
    scales = (math.sqrt(total_width), 1.0 / math.sqrt(total_width))
    q_right, triangle = call_factor(
        functools.partial(right_kernel, scales),
        [(image_rows, size), (size, size)],
        [gram_right, image],
    )
    return (q_left, q_right.reshape(1, image_rows, size), triangle)


def solution(mesh):
    fine = Mesh(mesh.devices.reshape(8, 4, 2, 8), ROW + ("col",))
    return jax.shard_map(
        per_device,
        mesh=fine,
        in_specs=(P(ROW, "col"), P("col", None)),
        out_specs=(P(ROW + ("col",), None), P("col", ROW, None), P()),
        check_vma=False,
    )
```

```python
import functools
import math

import jax
import jax.numpy as jnp
from jax import lax
from jax.experimental import pallas as pl
from jax.experimental.pallas import tpu as pltpu
from jax.sharding import Mesh
from jax.sharding import PartitionSpec as P

HIGHEST = lax.Precision.HIGHEST
BLOCK = 128
RANK = 8
ENOUGH = 0.05
ROW = ("y", "x", "core")


def across_lanes(piece, column):
    place = jnp.full(piece.shape, column, jnp.int32)
    return jnp.take_along_axis(piece, place, axis=1, mode="promise_in_bounds")


def across_rows(piece, row):
    return jnp.broadcast_to(piece[row : row + 1, :], piece.shape)


def eliminate(left, right, finished, first):
    row = lax.broadcasted_iota(jnp.int32, (8, BLOCK), 0)
    group, offset = divmod(first, 8)
    columns = [across_lanes(left[group], first + t) for t in range(RANK)]
    pivot = [[across_rows(columns[u], offset + t) for u in range(t + 1)] for t in range(RANK)]
    on_left = [across_rows(left[group], offset + t) for t in range(RANK)]
    on_right = [across_rows(right[group], offset + t) for t in range(RANK)]
    lower = [[None] * RANK for _ in range(RANK)]
    inverse = [None] * RANK
    for t in range(RANK):
        inverse[t] = 1.0 / pivot[t][t]
        for i in range(t + 1, RANK):
            lower[i][t] = pivot[i][t] * inverse[t]
        for i in range(t + 1, RANK):
            for j in range(t + 1, i + 1):
                pivot[i][j] = pivot[i][j] - lower[i][t] * pivot[j][t]
            on_left[i] = on_left[i] - lower[i][t] * on_left[t]
            on_right[i] = on_right[i] - lower[i][t] * on_right[t]
    back_left, back_right = [None] * RANK, [None] * RANK
    for t in reversed(range(RANK)):
        back_left[t] = on_left[t] * inverse[t]
        back_right[t] = on_right[t] * inverse[t]
        for s in reversed(range(t + 1, RANK)):
            back_left[t] = back_left[t] - lower[s][t] * back_left[s]
            back_right[t] = back_right[t] - lower[s][t] * back_right[s]
    for i in range(group, len(left)):
        if i == group and offset + RANK == 8:
            continue
        new_left, new_right = left[i], right[i]
        for t in reversed(range(RANK)):
            if i == group:
                factor = jnp.where(row >= offset + RANK, columns[t], 0.0)
            else:
                factor = across_lanes(left[i], first + t)
            new_left = new_left - factor * back_left[t]
            new_right = new_right - factor * back_right[t]
        left[i], right[i] = new_left, new_right
    for t in range(RANK):
        scaled = on_right[t] * lax.rsqrt(pivot[t][t])
        finished[group] = jnp.where(row == offset + t, scaled, finished[group])


def inverse_factors(blocks):
    groups = BLOCK // 8
    row = lax.broadcasted_iota(jnp.int32, (8, BLOCK), 0)
    lane = lax.broadcasted_iota(jnp.int32, (8, BLOCK), 1)
    states = []
    for block in blocks:
        left = [block[8 * i : 8 * i + 8, :] for i in range(groups)]
        right = [jnp.where(lane == row + 8 * i, 1.0, 0.0) for i in range(groups)]
        finished = [jnp.zeros((8, BLOCK), jnp.float32) for _ in range(groups)]
        states.append((left, right, finished))
    for first in range(0, BLOCK, RANK):
        for left, right, finished in states:
            eliminate(left, right, finished, first)
    return [jnp.concatenate(finished, axis=0) for _, _, finished in states]


def times_transposed(left, right):
    return lax.dot_general(
        left,
        right,
        (((1,), (1,)), ((), ())),
        precision=HIGHEST,
        preferred_element_type=jnp.float32,
    )


def factor_blocks(size, *problems):
    def step(index, carry):
        here = pl.ds(pl.multiple_of(index * BLOCK, BLOCK), BLOCK)
        found = inverse_factors([work[here, here] for work, _, _ in problems])
        for (_, _, inverse), value in zip(problems, found):
            inverse[...] = value
        for block in range(size // BLOCK):
            first, after = block * BLOCK, (block + 1) * BLOCK

            @pl.when(index == block)
            def _(first=first, after=after):
                for work, factor, inverse in problems:
                    panel = times_transposed(work[first:, first:after], inverse[...])
                    factor[first:, first:after] = panel
                    if after < size:
                        below, right = panel[BLOCK:], panel[BLOCK : size - first]
                        work[after:, after:] -= times_transposed(below, right)

        return carry

    lax.fori_loop(0, size // BLOCK, step, 0)


def diagonal(square, width):
    row = lax.broadcasted_iota(jnp.int32, (BLOCK, BLOCK), 0)
    column = lax.broadcasted_iota(jnp.int32, (BLOCK, BLOCK), 1)
    blocks = [
        jnp.where(row == column, square[i : i + BLOCK, i : i + BLOCK], 0.0)
        for i in range(0, width, BLOCK)
    ]
    return jnp.concatenate([jnp.sum(block, axis=1, keepdims=True) for block in blocks], axis=0)


def place_rows(which, grams_ref, work):
    for place in range(64):
        y, x, core = place // 8, place // 2 % 4, place % 2
        work[8 * place : 8 * place + 8, :] = grams_ref[core, x, which, 8 * y : 8 * y + 8, :]


def both_kernel(
    scales,
    grams_ref,
    own_ref,
    raw_ref,
    left_ref,
    right_ref,
    triangle_ref,
    margin_ref,
    work_left,
    factor_left,
    inverse_left,
    work_right,
    factor_right,
    inverse_right,
):
    size, own = own_ref.shape[1], own_ref.shape[0]
    place_rows(0, grams_ref, work_left)
    place_rows(1, grams_ref, work_right)
    before = [diagonal(work, size) for work in (work_left, work_right)]
    row = lax.broadcasted_iota(jnp.int32, (size, size), 0)
    column = lax.broadcasted_iota(jnp.int32, (size, size), 1)
    work_left[size : size + own, :] = own_ref[...]
    work_left[size + own :, :] = jnp.where(row == column, 1.0, 0.0)
    work_right[size:, :] = raw_ref[...]
    factor_blocks(
        size,
        (work_left, factor_left, inverse_left),
        (work_right, factor_right, inverse_right),
    )
    left_ref[...] = factor_left[size : size + own, :] * scales[0]
    right_ref[...] = factor_right[size:, :] * scales[1]

    turned = factor_left[size + own :, :] * scales[2]
    lower = jnp.where(row >= column, factor_right[:size, :], 0.0)
    half = size // 2
    triangle_ref[:half, :half] = gram_rows(turned[:half, :half], lower[:half, :half])
    triangle_ref[:half, half:] = jnp.zeros((half, size - half), jnp.float32)
    bottom = gram_rows(turned[:, half:], lower)
    keep = (row >= column)[half:]
    triangle_ref[half:, :] = jnp.where(keep, bottom, 0.0)
    top = triangle_ref[:half, :half]
    triangle_ref[:half, :half] = jnp.where((row >= column)[:half, :half], top, 0.0)

    after = [diagonal(factor, size) for factor in (factor_left, factor_right)]
    margin = 1.0
    for a, b in zip(after, before):
        share = a * a / b
        share = jnp.where((share > 0.0) & (share < 2.0), share, -1.0)
        margin = jnp.minimum(margin, jnp.min(share, axis=0, keepdims=True))
    margin_ref[...] = jnp.broadcast_to(margin, margin_ref.shape)


def sort_halves(image, image_ref):
    halves, rows, size = image_ref.shape
    image = image.reshape(rows // 16, halves, 16, size)
    for half in range(halves):
        image_ref[half] = image[:, half].reshape(rows, size)


def raw_kernel(turned_ref, sketch_ref, image_ref):
    sketch = sketch_ref[...]
    high = sketch.astype(jnp.bfloat16)
    low = (sketch - high.astype(jnp.float32)).astype(jnp.bfloat16)
    turned = turned_ref[...]
    image = jnp.dot(turned, high, preferred_element_type=jnp.float32)
    image += jnp.dot(turned, low, preferred_element_type=jnp.float32)
    sort_halves(image, image_ref)


def left_kernel(gram_ref, tall_ref, turned_ref, image_ref, work, factor, inverse):
    size = gram_ref.shape[0]
    for place in range(size // 8):
        y, x, core = place // 8, place // 2 % 4, place % 2
        came = (core * 4 + x) * 8 + y
        work[8 * place : 8 * place + 8, :] = gram_ref[8 * came : 8 * came + 8, :]
    work[size:, :] = tall_ref[...]
    factor_blocks(size, (work, factor, inverse))
    basis_half = factor[size:, :].astype(jnp.bfloat16)
    image = jnp.dot(turned_ref[...], basis_half, preferred_element_type=jnp.float32)
    sort_halves(image, image_ref)


def right_kernel(scales, gram_ref, tall_ref, solved_ref, lower_ref, work, factor, inverse):
    size = gram_ref.shape[0]
    work[:size, :] = gram_ref[...]
    work[size:, :] = tall_ref[...]
    factor_blocks(size, (work, factor, inverse))
    solved_ref[...] = factor[size:, :] * scales[0]
    row = lax.broadcasted_iota(jnp.int32, (size, size), 0)
    column = lax.broadcasted_iota(jnp.int32, (size, size), 1)
    lower_ref[...] = jnp.where(row >= column, factor[:size, :] * scales[1], 0.0)


def call(kernel, shapes, operands, extra=()):
    size = operands[1].shape[-1]
    scratch = []
    for rows in extra:
        held = pltpu.VMEM((size + rows, size), jnp.float32)
        scratch += [held, held, pltpu.VMEM((BLOCK, BLOCK), jnp.float32)]
    return pl.pallas_call(
        kernel,
        out_shape=[jax.ShapeDtypeStruct(shape, jnp.float32) for shape in shapes],
        in_specs=[pl.BlockSpec(memory_space=pltpu.VMEM)] * len(operands),
        out_specs=[pl.BlockSpec(memory_space=pltpu.VMEM)] * len(shapes),
        scratch_shapes=scratch,
        compiler_params=pltpu.CompilerParams(vmem_limit_bytes=40 * 2**20),
        cost_estimate=pl.CostEstimate(
            flops=2 * size**3, bytes_accessed=8 * size * size, transcendentals=size
        ),
    )(*operands)


def gather(piece, axes):
    copies = jnp.broadcast_to(piece[None], (lax.axis_size(axes),) + piece.shape)
    return lax.all_to_all(copies, axes, 0, 0, tiled=True)


def pack(values):
    power = jnp.clip(jnp.ceil(jnp.log2(jnp.max(jnp.abs(values)))), -100.0, 100.0)
    scaled = (values * jnp.exp2(14.0 - power)).astype(jnp.float16)
    lanes = jnp.full((*values.shape[:-1], 128), power, jnp.float16)
    return jnp.concatenate([scaled, lanes], axis=-1)


def unpack(message):
    size = message.shape[-1] - 128
    power = message[..., size : size + 1].astype(jnp.float32)
    return message[..., :size].astype(jnp.float32) * jnp.exp2(power - 14.0)


def gram_rows(left, right):
    return lax.dot_general(
        left,
        right,
        (((0,), (0,)), ((), ())),
        precision=HIGHEST,
        preferred_element_type=jnp.float32,
    )


def exchange_halves(partial_image):
    return jnp.sum(lax.all_to_all(partial_image, "core", 0, 0, tiled=True), axis=0)


def share_of_gram(rows):
    size = rows.shape[1]
    gram = gram_rows(rows, rows).reshape(size // 8, 8, size)
    share = lax.dynamic_index_in_dim(gram, lax.axis_index("col"), 1, keepdims=False)
    return share.reshape(size // 8, 4, size // 4)


def gather_gram(piece):
    size = piece.size
    eight = gather(piece, ("y", "col")).reshape(-1, size)
    four = gather(eight, ("x",)).reshape(-1, size)
    return gather(four, ("core",)).reshape(size, size)


def by_basis(gram_left, sketch, turned, scales):
    size, image_rows = sketch.shape[1], 16
    (partial_image,) = call(
        left_kernel,
        [(2, turned.shape[0] // 2, size)],
        [gram_left, sketch, turned],
        (sketch.shape[0],),
    )
    parts = exchange_halves(partial_image).astype(jnp.bfloat16).reshape(-1, image_rows, size)
    parts = lax.all_to_all(parts, ("y", "x"), 0, 0, tiled=True)
    image = jnp.sum(parts.astype(jnp.float32), axis=0)

    near = gather(image, ("x", "core")).reshape(-1, size)
    start = (lax.axis_index("core") * 4 + lax.axis_index("x")) * (size // 8)
    chosen = lax.dynamic_slice_in_dim(near, start, size // 8, 1)
    share = gram_rows(chosen, near).reshape(size // 8, 4, size // 4)
    share = lax.all_to_all(share, ("y", "col"), 0, 0, tiled=True)
    gram_right = gather_gram(jnp.sum(share, axis=0))
    q_right, triangle = call(
        functools.partial(right_kernel, scales),
        [(image_rows, size), (size, size)],
        [gram_right, image],
        (image_rows,),
    )
    return (q_right, triangle)


def per_device(hidden_states, sketch_matrix):
    rows, block_width = hidden_states.shape
    size = sketch_matrix.shape[1]
    cols, spread = lax.axis_size("col"), lax.axis_size(ROW)
    own_rows, image_rows = rows // cols, block_width // spread
    root_rows, root_width = math.sqrt(rows * spread), math.sqrt(block_width * cols)
    turned = hidden_states.T

    partial_sketch = jnp.dot(hidden_states, sketch_matrix, preferred_element_type=jnp.float32)
    parts = pack(partial_sketch).reshape(cols, own_rows, size + 128)
    own = jnp.sum(unpack(lax.all_to_all(parts, "col", 0, 0, tiled=True)), axis=0)
    sketch = unpack(gather(pack(own), "col")).reshape(rows, size)
    own = lax.dynamic_slice_in_dim(sketch, lax.axis_index("col") * own_rows, own_rows, 0)

    (partial_raw,) = call(raw_kernel, [(2, block_width // 2, size)], [turned, sketch])
    parts = pack(exchange_halves(partial_raw)).reshape(spread // 2, image_rows, size + 128)
    raw = jnp.sum(unpack(lax.all_to_all(parts, ("y", "x"), 0, 0, tiled=True)), axis=0)

    near = gather(raw, "col").reshape(-1, size)
    share = jnp.concatenate([share_of_gram(sketch), share_of_gram(near)], axis=1)
    share = jnp.sum(lax.all_to_all(share, ROW, 0, 0, tiled=True), axis=0)
    eight = gather(share, ("y", "col")).reshape(spread, 2, size)
    four = gather(jnp.swapaxes(eight, 0, 1), ("x",))
    grams = gather(four, ("core",))

    scales = (root_rows, root_width, 1.0 / root_width)
    q_left, q_right, triangle, margin = call(
        functools.partial(both_kernel, scales),
        [(own_rows, size), (image_rows, size), (size, size), (8, 128)],
        [grams, own, raw],
        (own_rows + size, image_rows),
    )
    q_right, triangle = lax.cond(
        margin[0, 0] > ENOUGH,
        lambda: (q_right, triangle),
        lambda: by_basis(grams[:, :, 0].reshape(size, size), sketch, turned, scales[1:]),
    )
    return (q_left, q_right.reshape(1, image_rows, size), triangle)


def solution(mesh):
    fine = Mesh(mesh.devices.reshape(8, 4, 2, 8), ROW + ("col",))
    return jax.shard_map(
        per_device,
        mesh=fine,
        in_specs=(P(ROW, "col"), P("col", None)),
        out_specs=(P(ROW + ("col",), None), P("col", ROW, None), P()),
        check_vma=False,
    )
```

```python
import functools
import math

import jax
import jax.numpy as jnp
from jax import lax
from jax.experimental import pallas as pl
from jax.experimental.pallas import tpu as pltpu
from jax.sharding import Mesh
from jax.sharding import PartitionSpec as P

HIGHEST = lax.Precision.HIGHEST
BLOCK = 128
ENOUGH = 0.05
ROW = ("y", "x", "core")


def across_lanes(piece, column):
    place = jnp.full(piece.shape, column, jnp.int32)
    return jnp.take_along_axis(piece, place, axis=1, mode="promise_in_bounds")


def across_rows(piece, row):
    return jnp.broadcast_to(piece[row : row + 1, :], piece.shape)


def eliminate(tiles, finished, group):
    row = lax.broadcasted_iota(jnp.int32, (8, BLOCK), 0)
    lane = lax.broadcasted_iota(jnp.int32, (8, BLOCK), 1) - 8 * group
    here = (lane >= 0) & (lane < 8)
    columns = [across_lanes(tiles[group], 8 * group + t) for t in range(8)]
    pivot = [[across_rows(columns[u], t) for u in range(t + 1)] for t in range(8)]
    head = jnp.where(here, jnp.where(lane == row, 1.0, 0.0), tiles[group])
    rows = [across_rows(head, t) for t in range(8)]
    lower = [[None] * 8 for _ in range(8)]
    inverse = [None] * 8
    for t in range(8):
        inverse[t] = 1.0 / pivot[t][t]
        for i in range(t + 1, 8):
            lower[i][t] = pivot[i][t] * inverse[t]
        for i in range(t + 1, 8):
            for j in range(t + 1, i + 1):
                pivot[i][j] = pivot[i][j] - lower[i][t] * pivot[j][t]
            rows[i] = rows[i] - lower[i][t] * rows[t]
    back = [None] * 8
    for t in reversed(range(8)):
        back[t] = rows[t] * inverse[t]
        for s in reversed(range(t + 1, 8)):
            back[t] = back[t] - lower[s][t] * back[s]
    for i in range(group + 1, len(tiles)):
        tile = jnp.where(here, 0.0, tiles[i])
        for t in reversed(range(8)):
            tile = tile - across_lanes(tiles[i], 8 * group + t) * back[t]
        tiles[i] = tile
    done = jnp.zeros((8, BLOCK), jnp.float32)
    for t in range(8):
        done = jnp.where(row == t, rows[t] * lax.rsqrt(pivot[t][t]), done)
    finished.append(jnp.where(lane < 8, done, 0.0))


def inverse_factors(blocks):
    groups = BLOCK // 8
    states = [([block[8 * i : 8 * i + 8, :] for i in range(groups)], []) for block in blocks]
    for group in range(groups):
        for tiles, finished in states:
            eliminate(tiles, finished, group)
    return [jnp.concatenate(finished, axis=0) for _, finished in states]


def times_transposed(left, right):
    return lax.dot_general(
        left,
        right,
        (((1,), (1,)), ((), ())),
        precision=HIGHEST,
        preferred_element_type=jnp.float32,
    )


def factor_blocks(size, *problems):
    def step(index, carry):
        here = pl.ds(pl.multiple_of(index * BLOCK, BLOCK), BLOCK)
        found = inverse_factors([work[here, here] for work, _, _, _ in problems])
        for (_, _, inverse, _), value in zip(problems, found):
            inverse[...] = value
        for block in range(size // BLOCK):
            first, after = block * BLOCK, (block + 1) * BLOCK

            @pl.when(index == block)
            def _(first=first, after=after):
                for work, factor, inverse, rows in problems:
                    last = min(rows + after, work.shape[0])
                    panel = times_transposed(work[first:last, first:after], inverse[...])
                    factor[first:last, first:after] = panel
                    if after < size:
                        below, right = panel[BLOCK:], panel[BLOCK : size - first]
                        work[after:last, after:] -= times_transposed(below, right)

        return carry

    lax.fori_loop(0, size // BLOCK, step, 0)


def diagonal(square, width):
    row = lax.broadcasted_iota(jnp.int32, (BLOCK, BLOCK), 0)
    column = lax.broadcasted_iota(jnp.int32, (BLOCK, BLOCK), 1)
    blocks = [
        jnp.where(row == column, square[i : i + BLOCK, i : i + BLOCK], 0.0)
        for i in range(0, width, BLOCK)
    ]
    return jnp.concatenate([jnp.sum(block, axis=1, keepdims=True) for block in blocks], axis=0)


def place_rows(grams_ref, work_left, work_right=None):
    for group in range(64):
        y, x, core = group // 8, group // 2 % 4, group % 2
        split = (group // 16 + 1) * BLOCK
        came = grams_ref[core, x, 8 * y : 8 * y + 8, :]
        work_left[8 * group : 8 * group + 8, :split] = came[:, :split]
        if work_right is not None:
            mirrored = 8 * (63 - group)
            work_right[mirrored : mirrored + 8, : came.shape[1] - split] = came[:, split:]


def both_kernel(
    scales,
    grams_ref,
    own_ref,
    raw_ref,
    left_ref,
    right_ref,
    triangle_ref,
    margin_ref,
    work_left,
    factor_left,
    inverse_left,
    work_right,
    factor_right,
    inverse_right,
):
    size, own = own_ref.shape[1], own_ref.shape[0]
    place_rows(grams_ref, work_left, work_right)
    before = [diagonal(work, size) for work in (work_left, work_right)]
    row = lax.broadcasted_iota(jnp.int32, (size, size), 0)
    column = lax.broadcasted_iota(jnp.int32, (size, size), 1)
    work_left[size : size + own, :] = own_ref[...]
    work_left[size + own :, :] = jnp.where(row == column, 1.0, 0.0)
    work_right[size:, :] = raw_ref[...]
    factor_blocks(
        size,
        (work_left, factor_left, inverse_left, size + own),
        (work_right, factor_right, inverse_right, work_right.shape[0]),
    )
    left_ref[...] = factor_left[size : size + own, :] * scales[0]
    right_ref[...] = factor_right[size:, :] * scales[1]

    turned = jnp.where(row <= column, factor_left[size + own :, :] * scales[2], 0.0)
    lower = jnp.where(row >= column, factor_right[:size, :], 0.0)
    half = size // 2
    triangle_ref[:half, :half] = gram_rows(turned[:half, :half], lower[:half, :half])
    triangle_ref[:half, half:] = jnp.zeros((half, size - half), jnp.float32)
    bottom = gram_rows(turned[:, half:], lower)
    keep = (row >= column)[half:]
    triangle_ref[half:, :] = jnp.where(keep, bottom, 0.0)
    top = triangle_ref[:half, :half]
    triangle_ref[:half, :half] = jnp.where((row >= column)[:half, :half], top, 0.0)

    after = [diagonal(factor, size) for factor in (factor_left, factor_right)]
    margin = 1.0
    for a, b in zip(after, before):
        share = a * a / b
        share = jnp.where((share > 0.0) & (share < 2.0), share, -1.0)
        margin = jnp.minimum(margin, jnp.min(share, axis=0, keepdims=True))
    margin_ref[...] = jnp.broadcast_to(margin, margin_ref.shape)


def sort_halves(image, image_ref):
    halves, rows, size = image_ref.shape
    image = image.reshape(rows // 16, halves, 16, size)
    for half in range(halves):
        image_ref[half] = image[:, half].reshape(rows, size)


def raw_kernel(turned_ref, sketch_ref, image_ref):
    sketch = sketch_ref[...]
    high = sketch.astype(jnp.bfloat16)
    low = (sketch - high.astype(jnp.float32)).astype(jnp.bfloat16)
    turned = turned_ref[...]
    image = jnp.dot(turned, high, preferred_element_type=jnp.float32)
    image += jnp.dot(turned, low, preferred_element_type=jnp.float32)
    sort_halves(image, image_ref)


def left_kernel(grams_ref, tall_ref, turned_ref, image_ref, work, factor, inverse):
    size = tall_ref.shape[1]
    place_rows(grams_ref, work)
    work[size:, :] = tall_ref[...]
    factor_blocks(size, (work, factor, inverse, work.shape[0]))
    basis_half = factor[size:, :].astype(jnp.bfloat16)
    image = jnp.dot(turned_ref[...], basis_half, preferred_element_type=jnp.float32)
    sort_halves(image, image_ref)


def right_kernel(scales, gram_ref, tall_ref, solved_ref, lower_ref, work, factor, inverse):
    size = gram_ref.shape[0]
    work[:size, :] = gram_ref[...]
    work[size:, :] = tall_ref[...]
    factor_blocks(size, (work, factor, inverse, work.shape[0]))
    solved_ref[...] = factor[size:, :] * scales[0]
    row = lax.broadcasted_iota(jnp.int32, (size, size), 0)
    column = lax.broadcasted_iota(jnp.int32, (size, size), 1)
    lower_ref[...] = jnp.where(row >= column, factor[:size, :] * scales[1], 0.0)


def share_kernel(col_ref, sketch_ref, near_ref, share_ref):
    size = sketch_ref.shape[1]
    groups = size // 8
    column = lax.broadcasted_iota(jnp.int32, (size, groups), 0)
    group = lax.broadcasted_iota(jnp.int32, (size, groups), 1)
    col = col_ref[0:1, :groups]

    def rows(values, order):
        chosen = jnp.where(column == 8 * order + col, 1.0, 0.0)
        chosen = jnp.dot(
            values, chosen, precision=HIGHEST, preferred_element_type=jnp.float32
        )
        return gram_rows(chosen, values)

    left = rows(sketch_ref[...], group)
    right = rows(near_ref[...], groups - 1 - group)
    for first in range(0, groups, 16):
        split = (first // 16 + 1) * BLOCK
        share_ref[first : first + 16, :split] = left[first : first + 16, :split]
        rest = share_ref.shape[1] - split
        share_ref[first : first + 16, split:] = right[first : first + 16, :rest]


def call(kernel, shapes, operands, extra=()):
    size = operands[1].shape[-1]
    scratch = []
    for rows in extra:
        held = pltpu.VMEM((size + rows, size), jnp.float32)
        scratch += [held, held, pltpu.VMEM((BLOCK, BLOCK), jnp.float32)]
    return pl.pallas_call(
        kernel,
        out_shape=[jax.ShapeDtypeStruct(shape, jnp.float32) for shape in shapes],
        in_specs=[pl.BlockSpec(memory_space=pltpu.VMEM)] * len(operands),
        out_specs=[pl.BlockSpec(memory_space=pltpu.VMEM)] * len(shapes),
        scratch_shapes=scratch,
        compiler_params=pltpu.CompilerParams(vmem_limit_bytes=40 * 2**20),
        cost_estimate=pl.CostEstimate(
            flops=2 * size**3, bytes_accessed=8 * size * size, transcendentals=size
        ),
    )(*operands)


def gather(piece, axes):
    copies = jnp.broadcast_to(piece[None], (lax.axis_size(axes),) + piece.shape)
    return lax.all_to_all(copies, axes, 0, 0, tiled=True)


def pack(values):
    power = jnp.clip(jnp.ceil(jnp.log2(jnp.max(jnp.abs(values)))), -100.0, 100.0)
    scaled = (values * jnp.exp2(14.0 - power)).astype(jnp.float16)
    lanes = jnp.full((*values.shape[:-1], 128), power, jnp.float16)
    return jnp.concatenate([scaled, lanes], axis=-1)


def unpack(message):
    size = message.shape[-1] - 128
    power = message[..., size : size + 1].astype(jnp.float32)
    return message[..., :size].astype(jnp.float32) * jnp.exp2(power - 14.0)


def gram_rows(left, right):
    return lax.dot_general(
        left,
        right,
        (((0,), (0,)), ((), ())),
        precision=HIGHEST,
        preferred_element_type=jnp.float32,
    )


def exchange_halves(partial_image):
    return jnp.sum(lax.all_to_all(partial_image, "core", 0, 0, tiled=True), axis=0)


def gather_gram(piece):
    size = piece.size
    eight = gather(piece, ("y", "col")).reshape(-1, size)
    four = gather(eight, ("x",)).reshape(-1, size)
    return gather(four, ("core",)).reshape(size, size)


def by_basis(grams, sketch, turned, scales):
    size, image_rows = sketch.shape[1], 16
    (partial_image,) = call(
        left_kernel,
        [(2, turned.shape[0] // 2, size)],
        [grams, sketch, turned],
        (sketch.shape[0],),
    )
    parts = exchange_halves(partial_image).astype(jnp.bfloat16).reshape(-1, image_rows, size)
    parts = lax.all_to_all(parts, ("y", "x"), 0, 0, tiled=True)
    image = jnp.sum(parts.astype(jnp.float32), axis=0)

    near = gather(image, ("x", "core")).reshape(-1, size)
    start = (lax.axis_index("core") * 4 + lax.axis_index("x")) * (size // 8)
    chosen = lax.dynamic_slice_in_dim(near, start, size // 8, 1)
    share = gram_rows(chosen, near).reshape(size // 8, 4, size // 4)
    share = lax.all_to_all(share, ("y", "col"), 0, 0, tiled=True)
    gram_right = gather_gram(jnp.sum(share, axis=0))
    q_right, triangle = call(
        functools.partial(right_kernel, scales),
        [(image_rows, size), (size, size)],
        [gram_right, image],
        (image_rows,),
    )
    return (q_right, triangle)


def per_device(hidden_states, sketch_matrix):
    rows, block_width = hidden_states.shape
    size = sketch_matrix.shape[1]
    cols, spread = lax.axis_size("col"), lax.axis_size(ROW)
    own_rows, image_rows = rows // cols, block_width // spread
    root_rows, root_width = math.sqrt(rows * spread), math.sqrt(block_width * cols)
    turned = hidden_states.T

    partial_sketch = jnp.dot(hidden_states, sketch_matrix, preferred_element_type=jnp.float32)
    parts = pack(partial_sketch).reshape(cols, own_rows, size + 128)
    own = jnp.sum(unpack(lax.all_to_all(parts, "col", 0, 0, tiled=True)), axis=0)
    sketch = unpack(gather(pack(own), "col")).reshape(rows, size)
    own = lax.dynamic_slice_in_dim(sketch, lax.axis_index("col") * own_rows, own_rows, 0)

    (partial_raw,) = call(raw_kernel, [(2, block_width // 2, size)], [turned, sketch])
    parts = pack(exchange_halves(partial_raw)).reshape(spread // 2, image_rows, size + 128)
    raw = jnp.sum(unpack(lax.all_to_all(parts, ("y", "x"), 0, 0, tiled=True)), axis=0)

    near = gather(raw, "col").reshape(-1, size)
    wide = size + BLOCK
    col = jnp.full((8, 128), lax.axis_index("col"), jnp.int32)
    (share,) = call(share_kernel, [(spread, wide)], [col, sketch, near])
    share = lax.all_to_all(share.reshape(spread, 1, wide), ROW, 0, 0, tiled=True)
    eight = gather(jnp.sum(share, axis=0), ("y", "col")).reshape(spread, wide)
    grams = gather(gather(eight, ("x",)), ("core",))

    scales = (root_rows, root_width, 1.0 / root_width)
    q_left, q_right, triangle, margin = call(
        functools.partial(both_kernel, scales),
        [(own_rows, size), (image_rows, size), (size, size), (8, 128)],
        [grams, own, raw],
        (own_rows + size, image_rows),
    )
    q_right, triangle = lax.cond(
        margin[0, 0] > ENOUGH,
        lambda: (q_right, triangle),
        lambda: by_basis(grams, sketch, turned, scales[1:]),
    )
    return (q_left, q_right.reshape(1, image_rows, size), triangle)


def solution(mesh):
    fine = Mesh(mesh.devices.reshape(8, 4, 2, 8), ROW + ("col",))
    return jax.shard_map(
        per_device,
        mesh=fine,
        in_specs=(P(ROW, "col"), P("col", None)),
        out_specs=(P(ROW + ("col",), None), P("col", ROW, None), P()),
        check_vma=False,
    )
```

```python
import functools
import math

import jax
import jax.numpy as jnp
from jax import lax
from jax.experimental import pallas as pl
from jax.experimental.pallas import tpu as pltpu
from jax.sharding import Mesh
from jax.sharding import PartitionSpec as P

HIGHEST = lax.Precision.HIGHEST
BLOCK = 128
ENOUGH = 0.05
LANES = 128
ROW = ("y", "x", "core")


def across_lanes(piece, column):
    place = jnp.full(piece.shape, column, jnp.int32)
    return jnp.take_along_axis(piece, place, axis=1, mode="promise_in_bounds")


def across_rows(piece, row):
    return jnp.broadcast_to(piece[row : row + 1, :], piece.shape)


def eliminate(tiles, finished, group):
    row = lax.broadcasted_iota(jnp.int32, (8, BLOCK), 0)
    lane = lax.broadcasted_iota(jnp.int32, (8, BLOCK), 1) - 8 * group
    here = (lane >= 0) & (lane < 8)
    columns = [across_lanes(tiles[group], 8 * group + t) for t in range(8)]
    pivot = [[across_rows(columns[u], t) for u in range(t + 1)] for t in range(8)]
    head = jnp.where(here, jnp.where(lane == row, 1.0, 0.0), tiles[group])
    rows = [across_rows(head, t) for t in range(8)]
    lower = [[None] * 8 for _ in range(8)]
    inverse = [None] * 8
    for t in range(8):
        inverse[t] = 1.0 / pivot[t][t]
        for i in range(t + 1, 8):
            lower[i][t] = pivot[i][t] * inverse[t]
        for i in range(t + 1, 8):
            for j in range(t + 1, i + 1):
                pivot[i][j] = pivot[i][j] - lower[i][t] * pivot[j][t]
            rows[i] = rows[i] - lower[i][t] * rows[t]
    back = [None] * 8
    for t in reversed(range(8)):
        back[t] = rows[t] * inverse[t]
        for s in reversed(range(t + 1, 8)):
            back[t] = back[t] - lower[s][t] * back[s]
    for i in range(group + 1, len(tiles)):
        tile = jnp.where(here, 0.0, tiles[i])
        for t in reversed(range(8)):
            tile = tile - across_lanes(tiles[i], 8 * group + t) * back[t]
        tiles[i] = tile
    done = jnp.zeros((8, BLOCK), jnp.float32)
    for t in range(8):
        done = jnp.where(row == t, rows[t] * lax.rsqrt(pivot[t][t]), done)
    finished.append(jnp.where(lane < 8, done, 0.0))


def inverse_factors(blocks):
    groups = BLOCK // 8
    states = [([block[8 * i : 8 * i + 8, :] for i in range(groups)], []) for block in blocks]
    for group in range(groups):
        for tiles, finished in states:
            eliminate(tiles, finished, group)
    return [jnp.concatenate(finished, axis=0) for _, finished in states]


def times_transposed(left, right):
    return lax.dot_general(
        left,
        right,
        (((1,), (1,)), ((), ())),
        precision=HIGHEST,
        preferred_element_type=jnp.float32,
    )


def factor_blocks(size, *problems):
    def step(index, carry):
        here = pl.ds(pl.multiple_of(index * BLOCK, BLOCK), BLOCK)
        found = inverse_factors([work[here, here] for work, _, _, _ in problems])
        for (_, _, inverse, _), value in zip(problems, found):
            inverse[...] = value
        for block in range(size // BLOCK):
            first, after = block * BLOCK, (block + 1) * BLOCK

            @pl.when(index == block)
            def _(first=first, after=after):
                for work, factor, inverse, rows in problems:
                    last = min(rows + after, work.shape[0])
                    panel = times_transposed(work[first:last, first:after], inverse[...])
                    factor[first:last, first:after] = panel
                    if after < size:
                        below, right = panel[BLOCK:], panel[BLOCK : size - first]
                        work[after:last, after:] -= times_transposed(below, right)

        return carry

    lax.fori_loop(0, size // BLOCK, step, 0)


def diagonal(square, width):
    row = lax.broadcasted_iota(jnp.int32, (BLOCK, BLOCK), 0)
    column = lax.broadcasted_iota(jnp.int32, (BLOCK, BLOCK), 1)
    blocks = [
        jnp.where(row == column, square[i : i + BLOCK, i : i + BLOCK], 0.0)
        for i in range(0, width, BLOCK)
    ]
    return jnp.concatenate([jnp.sum(block, axis=1, keepdims=True) for block in blocks], axis=0)


def place_rows(grams_ref, work_left, work_right=None):
    for group in range(64):
        y, x, core = group // 8, group // 2 % 4, group % 2
        split = (group // 16 + 1) * BLOCK
        came = grams_ref[core, x, 8 * y : 8 * y + 8, :]
        work_left[8 * group : 8 * group + 8, :split] = came[:, :split]
        if work_right is not None:
            mirrored = 8 * (63 - group)
            work_right[mirrored : mirrored + 8, : came.shape[1] - split] = came[:, split:]


def both_kernel(
    scales,
    grams_ref,
    own_ref,
    raw_ref,
    left_ref,
    right_ref,
    triangle_ref,
    margin_ref,
    work_left,
    factor_left,
    inverse_left,
    work_right,
    factor_right,
    inverse_right,
):
    size, own = own_ref.shape[1], own_ref.shape[0]
    place_rows(grams_ref, work_left, work_right)
    before = [diagonal(work, size) for work in (work_left, work_right)]
    row = lax.broadcasted_iota(jnp.int32, (size, size), 0)
    column = lax.broadcasted_iota(jnp.int32, (size, size), 1)
    work_left[size : size + own, :] = own_ref[...]
    work_left[size + own :, :] = jnp.where(row == column, 1.0, 0.0)
    work_right[size:, :] = raw_ref[...]
    factor_blocks(
        size,
        (work_left, factor_left, inverse_left, size + own),
        (work_right, factor_right, inverse_right, work_right.shape[0]),
    )
    left_ref[...] = factor_left[size : size + own, :] * scales[0]
    right_ref[...] = factor_right[size:, :] * scales[1]

    turned = jnp.where(row <= column, factor_left[size + own :, :] * scales[2], 0.0)
    lower = jnp.where(row >= column, factor_right[:size, :], 0.0)
    half = size // 2
    triangle_ref[:half, :half] = gram_rows(turned[:half, :half], lower[:half, :half])
    triangle_ref[:half, half:] = jnp.zeros((half, size - half), jnp.float32)
    bottom = gram_rows(turned[:, half:], lower)
    keep = (row >= column)[half:]
    triangle_ref[half:, :] = jnp.where(keep, bottom, 0.0)
    top = triangle_ref[:half, :half]
    triangle_ref[:half, :half] = jnp.where((row >= column)[:half, :half], top, 0.0)

    after = [diagonal(factor, size) for factor in (factor_left, factor_right)]
    margin = 1.0
    for a, b in zip(after, before):
        share = a * a / b
        share = jnp.where((share > 0.0) & (share < 2.0), share, -1.0)
        margin = jnp.minimum(margin, jnp.min(share, axis=0, keepdims=True))
    margin_ref[...] = jnp.broadcast_to(margin, margin_ref.shape)


def sort_halves(image, image_ref):
    halves, rows, size = image_ref.shape
    image = image.reshape(rows // 16, halves, 16, size)
    for half in range(halves):
        image_ref[half] = image[:, half].reshape(rows, size)


def pack(values, packed_ref):
    peak = jnp.max(jnp.max(jnp.abs(values), axis=0, keepdims=True), axis=1, keepdims=True)
    power = jnp.clip(jnp.ceil(jnp.log2(peak)), -100.0, 100.0)
    rows, size = values.shape
    packed_ref[:, :size] = values * jnp.exp2(14.0 - power)
    packed_ref[:, size:] = jnp.broadcast_to(power, (rows, LANES))


def unpack(packed):
    size = packed.shape[1] - LANES
    scale = jnp.exp2(packed[:, size:] - 14.0)
    return packed[:, :size] * jnp.concatenate([scale] * (size // LANES), axis=1)


def unpacked_sum(parts_ref):
    total = unpack(parts_ref[0])
    for part in range(1, parts_ref.shape[0]):
        total += unpack(parts_ref[part])
    return total


def sketch_kernel(hidden_ref, matrix_ref, packed_ref):
    values = jnp.dot(hidden_ref[...], matrix_ref[...], preferred_element_type=jnp.float32)
    pack(values, packed_ref)


def own_kernel(parts_ref, packed_ref):
    pack(unpacked_sum(parts_ref), packed_ref)


def raw_kernel(turned_ref, parts_ref, image_ref, sketch_ref):
    sketch = jnp.concatenate([unpack(parts_ref[i]) for i in range(parts_ref.shape[0])], axis=0)
    sketch_ref[...] = sketch
    high = sketch.astype(jnp.bfloat16)
    low = (sketch - high.astype(jnp.float32)).astype(jnp.bfloat16)
    turned = turned_ref[...]
    image = jnp.dot(turned, high, preferred_element_type=jnp.float32)
    image += jnp.dot(turned, low, preferred_element_type=jnp.float32)
    sort_halves(image, image_ref)


def halves_kernel(halves_ref, packed_ref):
    pack(halves_ref[0] + halves_ref[1], packed_ref)


def sum_kernel(parts_ref, sum_ref, copies_ref):
    total = unpacked_sum(parts_ref)
    sum_ref[...] = total
    for copy in range(copies_ref.shape[0]):
        copies_ref[copy] = total


def left_kernel(grams_ref, tall_ref, turned_ref, image_ref, work, factor, inverse):
    size = tall_ref.shape[1]
    place_rows(grams_ref, work)
    work[size:, :] = tall_ref[...]
    factor_blocks(size, (work, factor, inverse, work.shape[0]))
    basis_half = factor[size:, :].astype(jnp.bfloat16)
    image = jnp.dot(turned_ref[...], basis_half, preferred_element_type=jnp.float32)
    sort_halves(image, image_ref)


def right_kernel(scales, gram_ref, tall_ref, solved_ref, lower_ref, work, factor, inverse):
    size = gram_ref.shape[0]
    work[:size, :] = gram_ref[...]
    work[size:, :] = tall_ref[...]
    factor_blocks(size, (work, factor, inverse, work.shape[0]))
    solved_ref[...] = factor[size:, :] * scales[0]
    row = lax.broadcasted_iota(jnp.int32, (size, size), 0)
    column = lax.broadcasted_iota(jnp.int32, (size, size), 1)
    lower_ref[...] = jnp.where(row >= column, factor[:size, :] * scales[1], 0.0)


def share_kernel(col_ref, sketch_ref, near_ref, share_ref):
    size = sketch_ref.shape[1]
    groups = size // 8
    column = lax.broadcasted_iota(jnp.int32, (size, groups), 0)
    group = lax.broadcasted_iota(jnp.int32, (size, groups), 1)
    col = col_ref[0:1, :groups]

    def rows(values, order):
        chosen = jnp.where(column == 8 * order + col, 1.0, 0.0)
        chosen = jnp.dot(
            values, chosen, precision=HIGHEST, preferred_element_type=jnp.float32
        )
        return gram_rows(chosen, values)

    left = rows(sketch_ref[...], group)
    right = rows(near_ref[...], groups - 1 - group)
    for first in range(0, groups, 16):
        split = (first // 16 + 1) * BLOCK
        share_ref[first : first + 16, :split] = left[first : first + 16, :split]
        rest = share_ref.shape[1] - split
        share_ref[first : first + 16, split:] = right[first : first + 16, :rest]


def call(kernel, shapes, operands, extra=()):
    size = operands[1].shape[-1] if extra else 0
    scratch = []
    for rows in extra:
        held = pltpu.VMEM((size + rows, size), jnp.float32)
        scratch += [held, held, pltpu.VMEM((BLOCK, BLOCK), jnp.float32)]
    return pl.pallas_call(
        kernel,
        out_shape=[jax.ShapeDtypeStruct(shape, jnp.float32) for shape in shapes],
        in_specs=[pl.BlockSpec(memory_space=pltpu.VMEM)] * len(operands),
        out_specs=[pl.BlockSpec(memory_space=pltpu.VMEM)] * len(shapes),
        scratch_shapes=scratch,
        compiler_params=pltpu.CompilerParams(vmem_limit_bytes=40 * 2**20),
        cost_estimate=pl.CostEstimate(
            flops=1024 * math.prod(shapes[0]) + 2 * size**3,
            bytes_accessed=8 * math.prod(shapes[0]),
            transcendentals=size,
        ),
    )(*operands)


def gather(piece, axes):
    copies = jnp.broadcast_to(piece[None], (lax.axis_size(axes),) + piece.shape)
    return lax.all_to_all(copies, axes, 0, 0, tiled=True)


def gram_rows(left, right):
    return lax.dot_general(
        left,
        right,
        (((0,), (0,)), ((), ())),
        precision=HIGHEST,
        preferred_element_type=jnp.float32,
    )


def exchange_halves(partial_image):
    return jnp.sum(lax.all_to_all(partial_image, "core", 0, 0, tiled=True), axis=0)


def gather_gram(piece):
    size = piece.size
    eight = gather(piece, ("y", "col")).reshape(-1, size)
    four = gather(eight, ("x",)).reshape(-1, size)
    return gather(four, ("core",)).reshape(size, size)


def by_basis(grams, sketch, turned, scales):
    size, image_rows = sketch.shape[1], 16
    (partial_image,) = call(
        left_kernel,
        [(2, turned.shape[0] // 2, size)],
        [grams, sketch, turned],
        (sketch.shape[0],),
    )
    parts = exchange_halves(partial_image).astype(jnp.bfloat16).reshape(-1, image_rows, size)
    parts = lax.all_to_all(parts, ("y", "x"), 0, 0, tiled=True)
    image = jnp.sum(parts.astype(jnp.float32), axis=0)

    near = gather(image, ("x", "core")).reshape(-1, size)
    start = (lax.axis_index("core") * 4 + lax.axis_index("x")) * (size // 8)
    chosen = lax.dynamic_slice_in_dim(near, start, size // 8, 1)
    share = gram_rows(chosen, near).reshape(size // 8, 4, size // 4)
    share = lax.all_to_all(share, ("y", "col"), 0, 0, tiled=True)
    gram_right = gather_gram(jnp.sum(share, axis=0))
    q_right, triangle = call(
        functools.partial(right_kernel, scales),
        [(image_rows, size), (size, size)],
        [gram_right, image],
        (image_rows,),
    )
    return (q_right, triangle)


def per_device(hidden_states, sketch_matrix):
    rows, block_width = hidden_states.shape
    size = sketch_matrix.shape[1]
    cols, spread = lax.axis_size("col"), lax.axis_size(ROW)
    own_rows, image_rows = rows // cols, block_width // spread
    root_rows, root_width = math.sqrt(rows * spread), math.sqrt(block_width * cols)
    turned = hidden_states.T

    def halved(packed, axes, groups):
        packed = packed.astype(jnp.float16).reshape(groups, -1, size + LANES)
        return lax.all_to_all(packed, axes, 0, 0, tiled=True).astype(jnp.float32)

    packed_shape = (rows, size + LANES)
    (packed,) = call(sketch_kernel, [packed_shape], [hidden_states, sketch_matrix])
    parts = halved(packed, "col", cols)
    (packed,) = call(own_kernel, [(own_rows, size + LANES)], [parts])
    parts = gather(packed.astype(jnp.float16), "col").astype(jnp.float32)

    half = block_width // 2
    partial_raw, sketch = call(raw_kernel, [(2, half, size), (rows, size)], [turned, parts])
    own = lax.dynamic_slice_in_dim(sketch, lax.axis_index("col") * own_rows, own_rows, 0)
    halves = lax.all_to_all(partial_raw, "core", 0, 0, tiled=True)
    (packed,) = call(halves_kernel, [(half, size + LANES)], [halves])
    parts = halved(packed, ("y", "x"), spread // 2)
    raw, near = call(sum_kernel, [(image_rows, size), (cols, image_rows, size)], [parts])

    near = lax.all_to_all(near, "col", 0, 0, tiled=True).reshape(-1, size)
    wide = size + BLOCK
    col = jnp.full((8, 128), lax.axis_index("col"), jnp.int32)
    (share,) = call(share_kernel, [(spread, wide)], [col, sketch, near])
    share = lax.all_to_all(share.reshape(spread, 1, wide), ROW, 0, 0, tiled=True)
    eight = gather(jnp.sum(share, axis=0), ("y", "col")).reshape(spread, wide)
    grams = gather(gather(eight, ("x",)), ("core",))

    scales = (root_rows, root_width, 1.0 / root_width)
    q_left, q_right, triangle, margin = call(
        functools.partial(both_kernel, scales),
        [(own_rows, size), (image_rows, size), (size, size), (8, 128)],
        [grams, own, raw],
        (own_rows + size, image_rows),
    )
    q_right, triangle = lax.cond(
        margin[0, 0] > ENOUGH,
        lambda: (q_right, triangle),
        lambda: by_basis(grams, sketch, turned, scales[1:]),
    )
    return (q_left, q_right.reshape(1, image_rows, size), triangle)


def solution(mesh):
    fine = Mesh(mesh.devices.reshape(8, 4, 2, 8), ROW + ("col",))
    return jax.shard_map(
        per_device,
        mesh=fine,
        in_specs=(P(ROW, "col"), P("col", None)),
        out_specs=(P(ROW + ("col",), None), P("col", ROW, None), P()),
        check_vma=False,
    )
```

```python
import functools
import math

import jax
import jax.numpy as jnp
from jax import lax
from jax.experimental import pallas as pl
from jax.experimental.pallas import tpu as pltpu
from jax.sharding import Mesh
from jax.sharding import PartitionSpec as P

HIGHEST = lax.Precision.HIGHEST
BLOCK = 128
ENOUGH = 0.05
LANES = 128
TILES = 4
ROW = ("y", "x", "core")


def across_lanes(piece, column):
    place = jnp.full(piece.shape, column, jnp.int32)
    return jnp.take_along_axis(piece, place, axis=1, mode="promise_in_bounds")


def across_rows(piece, row):
    return jnp.broadcast_to(piece[row : row + 1, :], piece.shape)


def eliminate(tiles, finished, group):
    row = lax.broadcasted_iota(jnp.int32, (8, BLOCK), 0)
    lane = lax.broadcasted_iota(jnp.int32, (8, BLOCK), 1) - 8 * group
    here = (lane >= 0) & (lane < 8)
    columns = [across_lanes(tiles[group], 8 * group + t) for t in range(8)]
    pivot = [[across_rows(columns[u], t) for u in range(t + 1)] for t in range(8)]
    head = jnp.where(here, jnp.where(lane == row, 1.0, 0.0), tiles[group])
    rows = [across_rows(head, t) for t in range(8)]
    lower = [[None] * 8 for _ in range(8)]
    inverse = [None] * 8
    for t in range(8):
        inverse[t] = 1.0 / pivot[t][t]
        for i in range(t + 1, 8):
            lower[i][t] = pivot[i][t] * inverse[t]
        for i in range(t + 1, 8):
            for j in range(t + 1, i + 1):
                pivot[i][j] = pivot[i][j] - lower[i][t] * pivot[j][t]
            rows[i] = rows[i] - lower[i][t] * rows[t]
    back = [None] * 8
    for t in reversed(range(8)):
        back[t] = rows[t] * inverse[t]
        for s in reversed(range(t + 1, 8)):
            back[t] = back[t] - lower[s][t] * back[s]
    for i in range(group + 1, len(tiles)):
        tile = jnp.where(here, 0.0, tiles[i])
        for t in reversed(range(8)):
            tile = tile - across_lanes(tiles[i], 8 * group + t) * back[t]
        tiles[i] = tile
    done = jnp.zeros((8, BLOCK), jnp.float32)
    for t in range(8):
        done = jnp.where(row == t, rows[t] * lax.rsqrt(pivot[t][t]), done)
    finished.append(jnp.where(lane < 8, done, 0.0))


def inverse_factors(blocks):
    groups = BLOCK // 8
    states = [([block[8 * i : 8 * i + 8, :] for i in range(groups)], []) for block in blocks]
    for group in range(groups):
        for tiles, finished in states:
            eliminate(tiles, finished, group)
    return [jnp.concatenate(finished, axis=0) for _, finished in states]


def times_transposed(left, right):
    return lax.dot_general(
        left,
        right,
        (((1,), (1,)), ((), ())),
        precision=HIGHEST,
        preferred_element_type=jnp.float32,
    )


def factor_blocks(size, *problems):
    def step(index, carry):
        here = pl.ds(pl.multiple_of(index * BLOCK, BLOCK), BLOCK)
        found = inverse_factors([work[here, here] for work, _, _, _ in problems])
        for (_, _, inverse, _), value in zip(problems, found):
            inverse[...] = value
        for block in range(size // BLOCK):
            first, after = block * BLOCK, (block + 1) * BLOCK

            @pl.when(index == block)
            def _(first=first, after=after):
                for work, factor, inverse, rows in problems:
                    last = min(rows + after, work.shape[0])
                    panel = times_transposed(work[first:last, first:after], inverse[...])
                    factor[first:last, first:after] = panel
                    if after < size:
                        below, right = panel[BLOCK:], panel[BLOCK : size - first]
                        work[after:last, after:] -= times_transposed(below, right)

        return carry

    lax.fori_loop(0, size // BLOCK, step, 0)


def diagonal(square, width):
    row = lax.broadcasted_iota(jnp.int32, (BLOCK, BLOCK), 0)
    column = lax.broadcasted_iota(jnp.int32, (BLOCK, BLOCK), 1)
    blocks = [
        jnp.where(row == column, square[i : i + BLOCK, i : i + BLOCK], 0.0)
        for i in range(0, width, BLOCK)
    ]
    return jnp.concatenate([jnp.sum(block, axis=1, keepdims=True) for block in blocks], axis=0)


def place_rows(grams_ref, work_left, work_right=None):
    for group in range(64):
        y, x, core = group // 8, group // 2 % 4, group % 2
        split = (group // 16 + 1) * BLOCK
        came = grams_ref[core, x, 8 * y : 8 * y + 8, :]
        work_left[8 * group : 8 * group + 8, :split] = came[:, :split]
        if work_right is not None:
            mirrored = 8 * (63 - group)
            work_right[mirrored : mirrored + 8, : came.shape[1] - split] = came[:, split:]


def both_kernel(
    scales,
    grams_ref,
    own_ref,
    raw_ref,
    left_ref,
    right_ref,
    triangle_ref,
    margin_ref,
    work_left,
    factor_left,
    inverse_left,
    work_right,
    factor_right,
    inverse_right,
):
    size, own = own_ref.shape[1], own_ref.shape[0]
    place_rows(grams_ref, work_left, work_right)
    before = [diagonal(work, size) for work in (work_left, work_right)]
    row = lax.broadcasted_iota(jnp.int32, (size, size), 0)
    column = lax.broadcasted_iota(jnp.int32, (size, size), 1)
    work_left[size : size + own, :] = own_ref[...]
    work_left[size + own :, :] = jnp.where(row == column, 1.0, 0.0)
    work_right[size:, :] = raw_ref[...]
    factor_blocks(
        size,
        (work_left, factor_left, inverse_left, size + own),
        (work_right, factor_right, inverse_right, work_right.shape[0]),
    )
    left_ref[...] = factor_left[size : size + own, :] * scales[0]
    right_ref[...] = factor_right[size:, :] * scales[1]

    turned = jnp.where(row <= column, factor_left[size + own :, :] * scales[2], 0.0)
    lower = jnp.where(row >= column, factor_right[:size, :], 0.0)
    half = size // 2
    triangle_ref[:half, :half] = gram_rows(turned[:half, :half], lower[:half, :half])
    triangle_ref[:half, half:] = jnp.zeros((half, size - half), jnp.float32)
    bottom = gram_rows(turned[:, half:], lower)
    keep = (row >= column)[half:]
    triangle_ref[half:, :] = jnp.where(keep, bottom, 0.0)
    top = triangle_ref[:half, :half]
    triangle_ref[:half, :half] = jnp.where((row >= column)[:half, :half], top, 0.0)

    after = [diagonal(factor, size) for factor in (factor_left, factor_right)]
    margin = 1.0
    for a, b in zip(after, before):
        share = a * a / b
        share = jnp.where((share > 0.0) & (share < 2.0), share, -1.0)
        margin = jnp.minimum(margin, jnp.min(share, axis=0, keepdims=True))
    margin_ref[0, 0] = margin[0, 0]


def sort_halves(image, image_ref):
    halves, rows, size = image_ref.shape
    image = image.reshape(rows // 16, halves, 16, size)
    for half in range(halves):
        image_ref[half] = image[:, half].reshape(rows, size)


def pack(values, packed_ref):
    peak = jnp.max(jnp.max(jnp.abs(values), axis=0, keepdims=True), axis=1, keepdims=True)
    power = jnp.clip(jnp.ceil(jnp.log2(peak)), -100.0, 100.0)
    values = values * jnp.exp2(14.0 - power)
    messages, length, _ = packed_ref.shape
    tiles = values.shape[1] // LANES
    rows = (length - 8) // tiles
    for message in range(messages):
        part = values[(message * rows) % values.shape[0] :][:rows]
        for tile in range(tiles):
            columns = part[:, LANES * tile : LANES * (tile + 1)]
            packed_ref[message, rows * tile : rows * (tile + 1), :] = columns
        packed_ref[message, tiles * rows :, :] = jnp.broadcast_to(power, (8, LANES))


def unpack(packed):
    length = packed.shape[0] - 8
    scaled = packed[:length] * jnp.exp2(packed[length : length + 1] - 14.0)
    rows = length // TILES
    return jnp.concatenate([scaled[rows * i : rows * (i + 1)] for i in range(TILES)], axis=1)


def unpacked_sum(parts_ref):
    total = unpack(parts_ref[0])
    for part in range(1, parts_ref.shape[0]):
        total += unpack(parts_ref[part])
    return total


def unpacked_rows(parts_ref):
    return jnp.concatenate([unpack(parts_ref[i]) for i in range(parts_ref.shape[0])], axis=0)


def sketch_kernel(hidden_ref, matrix_ref, packed_ref):
    values = jnp.dot(hidden_ref[...], matrix_ref[...], preferred_element_type=jnp.float32)
    pack(values, packed_ref)


def own_kernel(parts_ref, packed_ref):
    pack(unpacked_sum(parts_ref), packed_ref)


def raw_kernel(turned_ref, parts_ref, image_ref, sketch_ref):
    sketch = unpacked_rows(parts_ref)
    sketch_ref[...] = sketch
    high = sketch.astype(jnp.bfloat16)
    low = (sketch - high.astype(jnp.float32)).astype(jnp.bfloat16)
    turned = turned_ref[...]
    image = jnp.dot(turned, high, preferred_element_type=jnp.float32)
    image += jnp.dot(turned, low, preferred_element_type=jnp.float32)
    sort_halves(image, image_ref)


def halves_kernel(halves_ref, packed_ref):
    pack(halves_ref[0] + halves_ref[1], packed_ref)


def left_kernel(grams_ref, tall_ref, turned_ref, image_ref, work, factor, inverse):
    size = tall_ref.shape[1]
    place_rows(grams_ref, work)
    work[size:, :] = tall_ref[...]
    factor_blocks(size, (work, factor, inverse, work.shape[0]))
    basis_half = factor[size:, :].astype(jnp.bfloat16)
    image = jnp.dot(turned_ref[...], basis_half, preferred_element_type=jnp.float32)
    sort_halves(image, image_ref)


def right_kernel(scales, gram_ref, tall_ref, solved_ref, lower_ref, work, factor, inverse):
    size = gram_ref.shape[0]
    work[:size, :] = gram_ref[...]
    work[size:, :] = tall_ref[...]
    factor_blocks(size, (work, factor, inverse, work.shape[0]))
    solved_ref[...] = factor[size:, :] * scales[0]
    row = lax.broadcasted_iota(jnp.int32, (size, size), 0)
    column = lax.broadcasted_iota(jnp.int32, (size, size), 1)
    lower_ref[...] = jnp.where(row >= column, factor[:size, :] * scales[1], 0.0)


def chosen_gram_rows(values, col_ref, mirrored):
    size = values.shape[1]
    groups = size // 8
    column = lax.broadcasted_iota(jnp.int32, (size, groups), 0)
    group = lax.broadcasted_iota(jnp.int32, (size, groups), 1)
    if mirrored:
        group = groups - 1 - group
    chosen = jnp.where(column == 8 * group + col_ref[0:1, :groups], 1.0, 0.0)
    chosen = jnp.dot(values, chosen, precision=HIGHEST, preferred_element_type=jnp.float32)
    return gram_rows(chosen, values)


def left_share_kernel(col_ref, sketch_ref, left_ref):
    left_ref[...] = chosen_gram_rows(sketch_ref[...], col_ref, False)


def share_kernel(col_ref, left_ref, parts_ref, share_ref, near_ref):
    near = unpacked_rows(parts_ref)
    near_ref[...] = near
    right = chosen_gram_rows(near, col_ref, True)
    for first in range(0, share_ref.shape[0], 16):
        split = (first // 16 + 1) * BLOCK
        share_ref[first : first + 16, :split] = left_ref[first : first + 16, :split]
        rest = share_ref.shape[1] - split
        share_ref[first : first + 16, split:] = right[first : first + 16, :rest]


def call(kernel, shapes, operands, extra=()):
    size = operands[1].shape[-1] if extra else 0
    scratch = []
    for rows in extra:
        held = pltpu.VMEM((size + rows, size), jnp.float32)
        scratch += [held, held, pltpu.VMEM((BLOCK, BLOCK), jnp.float32)]
    return pl.pallas_call(
        kernel,
        out_shape=[jax.ShapeDtypeStruct(shape, jnp.float32) for shape in shapes],
        in_specs=[pl.BlockSpec(memory_space=pltpu.VMEM)] * len(operands),
        out_specs=[
            pl.BlockSpec(memory_space=pltpu.SMEM if shape == (1, 1) else pltpu.VMEM)
            for shape in shapes
        ],
        scratch_shapes=scratch,
        compiler_params=pltpu.CompilerParams(vmem_limit_bytes=40 * 2**20),
        cost_estimate=pl.CostEstimate(
            flops=1024 * math.prod(shapes[0]) + 2 * size**3,
            bytes_accessed=8 * math.prod(shapes[0]),
            transcendentals=size,
        ),
    )(*operands)


def gather(piece, axes):
    copies = jnp.broadcast_to(piece[None], (lax.axis_size(axes),) + piece.shape)
    return lax.all_to_all(copies, axes, 0, 0, tiled=True)


def gram_rows(left, right):
    return lax.dot_general(
        left,
        right,
        (((0,), (0,)), ((), ())),
        precision=HIGHEST,
        preferred_element_type=jnp.float32,
    )


def exchange_halves(partial_image):
    return jnp.sum(lax.all_to_all(partial_image, "core", 0, 0, tiled=True), axis=0)


def gather_gram(piece):
    size = piece.size
    eight = gather(piece, ("y", "col")).reshape(-1, size)
    four = gather(eight, ("x",)).reshape(-1, size)
    return gather(four, ("core",)).reshape(size, size)


def by_basis(grams, sketch, turned, scales):
    size, image_rows = sketch.shape[1], 16
    (partial_image,) = call(
        left_kernel,
        [(2, turned.shape[0] // 2, size)],
        [grams, sketch, turned],
        (sketch.shape[0],),
    )
    parts = exchange_halves(partial_image).astype(jnp.bfloat16).reshape(-1, image_rows, size)
    parts = lax.all_to_all(parts, ("y", "x"), 0, 0, tiled=True)
    image = jnp.sum(parts.astype(jnp.float32), axis=0)

    near = gather(image, ("x", "core")).reshape(-1, size)
    start = (lax.axis_index("core") * 4 + lax.axis_index("x")) * (size // 8)
    chosen = lax.dynamic_slice_in_dim(near, start, size // 8, 1)
    share = gram_rows(chosen, near).reshape(size // 8, 4, size // 4)
    share = lax.all_to_all(share, ("y", "col"), 0, 0, tiled=True)
    gram_right = gather_gram(jnp.sum(share, axis=0))
    q_right, triangle = call(
        functools.partial(right_kernel, scales),
        [(image_rows, size), (size, size)],
        [gram_right, image],
        (image_rows,),
    )
    return (q_right, triangle)


def per_device(hidden_states, sketch_matrix):
    rows, block_width = hidden_states.shape
    size = sketch_matrix.shape[1]
    cols, spread = lax.axis_size("col"), lax.axis_size(ROW)
    own_rows, image_rows = rows // cols, block_width // spread
    root_rows, root_width = math.sqrt(rows * spread), math.sqrt(block_width * cols)
    turned = hidden_states.T

    def halved(packed, axes):
        packed = packed.astype(jnp.float16)
        return lax.all_to_all(packed, axes, 0, 0, tiled=True).astype(jnp.float32)

    many, few = TILES * own_rows + 8, TILES * image_rows + 8
    (packed,) = call(sketch_kernel, [(cols, many, LANES)], [hidden_states, sketch_matrix])
    (packed,) = call(own_kernel, [(cols, many, LANES)], [halved(packed, "col")])
    parts = halved(packed, "col")

    half = block_width // 2
    partial_raw, sketch = call(raw_kernel, [(2, half, size), (rows, size)], [turned, parts])
    column = lax.axis_index("col")
    own = lax.dynamic_slice_in_dim(sketch, column * own_rows, own_rows, 0)
    halves = lax.all_to_all(partial_raw, "core", 0, 0, tiled=True)
    (packed,) = call(halves_kernel, [(spread // 2, few, LANES)], [halves])
    (packed,) = call(own_kernel, [(cols, few, LANES)], [halved(packed, ("y", "x"))])
    parts = halved(packed, "col")

    wide = size + BLOCK
    col = jnp.full((8, 128), column, jnp.int32)
    (left,) = call(left_share_kernel, [(spread, size)], [col, sketch])
    share, near = call(share_kernel, [(spread, wide), (cols * image_rows, size)], [col, left, parts])
    raw = lax.dynamic_slice_in_dim(near, column * image_rows, image_rows, 0)
    share = lax.all_to_all(share.reshape(spread, 1, wide), ROW, 0, 0, tiled=True)
    eight = gather(jnp.sum(share, axis=0), ("y", "col")).reshape(spread, wide)
    grams = gather(gather(eight, ("x",)), ("core",))

    scales = (root_rows, root_width, 1.0 / root_width)
    q_left, q_right, triangle, margin = call(
        functools.partial(both_kernel, scales),
        [(own_rows, size), (image_rows, size), (size, size), (1, 1)],
        [grams, own, raw],
        (own_rows + size, image_rows),
    )
    q_right, triangle = lax.cond(
        margin[0, 0] > ENOUGH,
        lambda: (q_right, triangle),
        lambda: by_basis(grams, sketch, turned, scales[1:]),
    )
    return (q_left, q_right.reshape(1, image_rows, size), triangle)


def solution(mesh):
    fine = Mesh(mesh.devices.reshape(8, 4, 2, 8), ROW + ("col",))
    return jax.shard_map(
        per_device,
        mesh=fine,
        in_specs=(P(ROW, "col"), P("col", None)),
        out_specs=(P(ROW + ("col",), None), P("col", ROW, None), P()),
        check_vma=False,
    )
```

```python
import functools
import math

import jax
import jax.numpy as jnp
from jax import lax
from jax.experimental import pallas as pl
from jax.experimental.pallas import tpu as pltpu
from jax.sharding import Mesh
from jax.sharding import PartitionSpec as P

HIGHEST = lax.Precision.HIGHEST
BLOCK = 128
ENOUGH = 0.05
LANES = 128
SPAN = 8
TILES = 4
ROW = ("y", "x", "core")


def across_lanes(piece, column):
    place = jnp.full(piece.shape, column, jnp.int32)
    return jnp.take_along_axis(piece, place, axis=1, mode="promise_in_bounds")


def across_rows(piece, row):
    return jnp.broadcast_to(piece[row : row + 1, :], piece.shape)


def eliminate(tiles, finished, group):
    row = lax.broadcasted_iota(jnp.int32, (8, BLOCK), 0)
    lane = lax.broadcasted_iota(jnp.int32, (8, BLOCK), 1) - 8 * group
    here = (lane >= 0) & (lane < 8)
    columns = [across_lanes(tiles[group], 8 * group + t) for t in range(8)]
    pivot = [[across_rows(columns[u], t) for u in range(t + 1)] for t in range(8)]
    head = jnp.where(here, jnp.where(lane == row, 1.0, 0.0), tiles[group])
    rows = [across_rows(head, t) for t in range(8)]
    lower = [[None] * 8 for _ in range(8)]
    inverse = [None] * 8
    for t in range(8):
        inverse[t] = 1.0 / pivot[t][t]
        for i in range(t + 1, 8):
            lower[i][t] = pivot[i][t] * inverse[t]
        for i in range(t + 1, 8):
            for j in range(t + 1, i + 1):
                pivot[i][j] = pivot[i][j] - lower[i][t] * pivot[j][t]
            rows[i] = rows[i] - lower[i][t] * rows[t]
    back = [None] * 8
    for t in reversed(range(8)):
        back[t] = rows[t] * inverse[t]
        for s in reversed(range(t + 1, 8)):
            back[t] = back[t] - lower[s][t] * back[s]
    for i in range(group + 1, (group // SPAN + 1) * SPAN):
        tile = jnp.where(here, 0.0, tiles[i])
        for t in reversed(range(8)):
            tile = tile - across_lanes(tiles[i], 8 * group + t) * back[t]
        tiles[i] = tile
    done = jnp.zeros((8, BLOCK), jnp.float32)
    for t in range(8):
        done = jnp.where(row == t, rows[t] * lax.rsqrt(pivot[t][t]), done)
    finished.append(jnp.where(lane < 8, done, 0.0))
    return done


def inverse_factors(blocks):
    groups = BLOCK // 8
    states = [([block[8 * i : 8 * i + 8, :] for i in range(groups)], []) for block in blocks]
    lane = lax.broadcasted_iota(jnp.int32, (8, BLOCK), 1)
    for start in range(0, groups, SPAN):
        stop = start + SPAN
        whole = [[] for _ in states]
        for group in range(start, stop):
            for (tiles, finished), kept in zip(states, whole):
                kept.append(eliminate(tiles, finished, group))
        if stop == groups:
            break
        later = lane >= 8 * stop
        for (tiles, finished), kept in zip(states, whole):
            kept = [jnp.where(later, k, f) for k, f in zip(kept, finished[start:])]
            kept = jnp.concatenate(kept, axis=0)
            change = gram_rows(kept, kept)
            for i in range(stop, groups):
                tile = jnp.where((lane >= 8 * start) & ~later, 0.0, tiles[i])
                tiles[i] = tile - change[8 * i : 8 * i + 8, :]
    return [jnp.concatenate(finished, axis=0) for _, finished in states]


def times_transposed(left, right):
    return lax.dot_general(
        left,
        right,
        (((1,), (1,)), ((), ())),
        precision=HIGHEST,
        preferred_element_type=jnp.float32,
    )


def factor_blocks(size, *problems):
    def step(index, carry):
        here = pl.ds(pl.multiple_of(index * BLOCK, BLOCK), BLOCK)
        found = inverse_factors([work[here, here] for work, _, _, _ in problems])
        for (_, _, inverse, _), value in zip(problems, found):
            inverse[...] = value
        for block in range(size // BLOCK):
            first, after = block * BLOCK, (block + 1) * BLOCK

            @pl.when(index == block)
            def _(first=first, after=after):
                for work, factor, inverse, rows in problems:
                    last = min(rows + after, work.shape[0])
                    panel = times_transposed(work[first:last, first:after], inverse[...])
                    factor[first:last, first:after] = panel
                    if after < size:
                        below, right = panel[BLOCK:], panel[BLOCK : size - first]
                        work[after:last, after:] -= times_transposed(below, right)

        return carry

    lax.fori_loop(0, size // BLOCK, step, 0)


def diagonal(square, width):
    row = lax.broadcasted_iota(jnp.int32, (BLOCK, BLOCK), 0)
    column = lax.broadcasted_iota(jnp.int32, (BLOCK, BLOCK), 1)
    blocks = [
        jnp.where(row == column, square[i : i + BLOCK, i : i + BLOCK], 0.0)
        for i in range(0, width, BLOCK)
    ]
    return jnp.concatenate([jnp.sum(block, axis=1, keepdims=True) for block in blocks], axis=0)


def place_rows(grams_ref, work_left, work_right=None):
    for group in range(64):
        y, x, core = group // 8, group // 2 % 4, group % 2
        split = (group // 16 + 1) * BLOCK
        came = grams_ref[core, x, 8 * y : 8 * y + 8, :]
        work_left[8 * group : 8 * group + 8, :split] = came[:, :split]
        if work_right is not None:
            mirrored = 8 * (63 - group)
            work_right[mirrored : mirrored + 8, : came.shape[1] - split] = came[:, split:]


def both_kernel(
    scales,
    grams_ref,
    own_ref,
    raw_ref,
    left_ref,
    right_ref,
    triangle_ref,
    margin_ref,
    work_left,
    factor_left,
    inverse_left,
    work_right,
    factor_right,
    inverse_right,
):
    size, own = own_ref.shape[1], own_ref.shape[0]
    place_rows(grams_ref, work_left, work_right)
    before = [diagonal(work, size) for work in (work_left, work_right)]
    row = lax.broadcasted_iota(jnp.int32, (size, size), 0)
    column = lax.broadcasted_iota(jnp.int32, (size, size), 1)
    work_left[size : size + own, :] = own_ref[...]
    work_left[size + own :, :] = jnp.where(row == column, 1.0, 0.0)
    work_right[size:, :] = raw_ref[...]
    factor_blocks(
        size,
        (work_left, factor_left, inverse_left, size + own),
        (work_right, factor_right, inverse_right, work_right.shape[0]),
    )
    left_ref[...] = factor_left[size : size + own, :] * scales[0]
    right_ref[...] = factor_right[size:, :] * scales[1]

    turned = jnp.where(row <= column, factor_left[size + own :, :] * scales[2], 0.0)
    lower = jnp.where(row >= column, factor_right[:size, :], 0.0)
    half = size // 2
    triangle_ref[:half, :half] = gram_rows(turned[:half, :half], lower[:half, :half])
    triangle_ref[:half, half:] = jnp.zeros((half, size - half), jnp.float32)
    bottom = gram_rows(turned[:, half:], lower)
    keep = (row >= column)[half:]
    triangle_ref[half:, :] = jnp.where(keep, bottom, 0.0)
    top = triangle_ref[:half, :half]
    triangle_ref[:half, :half] = jnp.where((row >= column)[:half, :half], top, 0.0)

    after = [diagonal(factor, size) for factor in (factor_left, factor_right)]
    margin = 1.0
    for a, b in zip(after, before):
        share = a * a / b
        share = jnp.where((share > 0.0) & (share < 2.0), share, -1.0)
        margin = jnp.minimum(margin, jnp.min(share, axis=0, keepdims=True))
    margin_ref[0, 0] = margin[0, 0]


def sort_halves(image, image_ref):
    halves, rows, size = image_ref.shape
    image = image.reshape(rows // 16, halves, 16, size)
    for half in range(halves):
        image_ref[half] = image[:, half].reshape(rows, size)


def pack(values, packed_ref):
    peak = jnp.max(jnp.max(jnp.abs(values), axis=0, keepdims=True), axis=1, keepdims=True)
    power = jnp.clip(jnp.ceil(jnp.log2(peak)), -100.0, 100.0)
    values = values * jnp.exp2(14.0 - power)
    messages, length, _ = packed_ref.shape
    tiles = values.shape[1] // LANES
    rows = (length - 8) // tiles
    for message in range(messages):
        part = values[(message * rows) % values.shape[0] :][:rows]
        for tile in range(tiles):
            columns = part[:, LANES * tile : LANES * (tile + 1)]
            packed_ref[message, rows * tile : rows * (tile + 1), :] = columns
        packed_ref[message, tiles * rows :, :] = jnp.broadcast_to(power, (8, LANES))


def unpack(packed):
    length = packed.shape[0] - 8
    scaled = packed[:length] * jnp.exp2(packed[length : length + 1] - 14.0)
    rows = length // TILES
    return jnp.concatenate([scaled[rows * i : rows * (i + 1)] for i in range(TILES)], axis=1)


def unpacked_sum(parts_ref):
    total = unpack(parts_ref[0])
    for part in range(1, parts_ref.shape[0]):
        total += unpack(parts_ref[part])
    return total


def unpacked_rows(parts_ref):
    return jnp.concatenate([unpack(parts_ref[i]) for i in range(parts_ref.shape[0])], axis=0)


def sketch_kernel(hidden_any, matrix_any, packed_ref, hidden, matrix, arrived):
    pieces = arrived.shape[0]
    width = hidden.shape[1] // pieces
    copies = []
    for piece in range(pieces):
        part = pl.ds(piece * width, width)
        copies.append(
            (
                pltpu.make_async_copy(hidden_any.at[:, part], hidden.at[:, part], arrived.at[piece, 0]),
                pltpu.make_async_copy(matrix_any.at[part, :], matrix.at[part, :], arrived.at[piece, 1]),
            )
        )
    for pair in copies:
        for copy in pair:
            copy.start()
    values = 0.0
    for piece, pair in enumerate(copies):
        for copy in pair:
            copy.wait()
        part = slice(piece * width, (piece + 1) * width)
        values += jnp.dot(hidden[:, part], matrix[part, :], preferred_element_type=jnp.float32)
    pack(values, packed_ref)


def own_kernel(parts_ref, packed_ref):
    pack(unpacked_sum(parts_ref), packed_ref)


def raw_kernel(turned_ref, parts_ref, image_ref, sketch_ref):
    sketch = unpacked_rows(parts_ref)
    sketch_ref[...] = sketch
    high = sketch.astype(jnp.bfloat16)
    low = (sketch - high.astype(jnp.float32)).astype(jnp.bfloat16)
    turned = turned_ref[...]
    image = jnp.dot(turned, high, preferred_element_type=jnp.float32)
    image += jnp.dot(turned, low, preferred_element_type=jnp.float32)
    sort_halves(image, image_ref)


def halves_kernel(halves_ref, packed_ref):
    pack(halves_ref[0] + halves_ref[1], packed_ref)


def left_kernel(grams_ref, tall_ref, turned_ref, image_ref, work, factor, inverse):
    size = tall_ref.shape[1]
    place_rows(grams_ref, work)
    work[size:, :] = tall_ref[...]
    factor_blocks(size, (work, factor, inverse, work.shape[0]))
    basis_half = factor[size:, :].astype(jnp.bfloat16)
    image = jnp.dot(turned_ref[...], basis_half, preferred_element_type=jnp.float32)
    sort_halves(image, image_ref)


def right_kernel(scales, gram_ref, tall_ref, solved_ref, lower_ref, work, factor, inverse):
    size = gram_ref.shape[0]
    work[:size, :] = gram_ref[...]
    work[size:, :] = tall_ref[...]
    factor_blocks(size, (work, factor, inverse, work.shape[0]))
    solved_ref[...] = factor[size:, :] * scales[0]
    row = lax.broadcasted_iota(jnp.int32, (size, size), 0)
    column = lax.broadcasted_iota(jnp.int32, (size, size), 1)
    lower_ref[...] = jnp.where(row >= column, factor[:size, :] * scales[1], 0.0)


def chosen_gram_rows(values, col_ref, mirrored):
    size = values.shape[1]
    groups = size // 8
    column = lax.broadcasted_iota(jnp.int32, (size, groups), 0)
    group = lax.broadcasted_iota(jnp.int32, (size, groups), 1)
    if mirrored:
        group = groups - 1 - group
    chosen = jnp.where(column == 8 * group + col_ref[0:1, :groups], 1.0, 0.0)
    chosen = jnp.dot(values, chosen, precision=HIGHEST, preferred_element_type=jnp.float32)
    return gram_rows(chosen, values)


def left_share_kernel(col_ref, sketch_ref, left_ref):
    left_ref[...] = chosen_gram_rows(sketch_ref[...], col_ref, False)


def share_kernel(col_ref, left_ref, parts_ref, share_ref, near_ref):
    near = unpacked_rows(parts_ref)
    near_ref[...] = near
    right = chosen_gram_rows(near, col_ref, True)
    for first in range(0, share_ref.shape[0], 16):
        split = (first // 16 + 1) * BLOCK
        share_ref[first : first + 16, :split] = left_ref[first : first + 16, :split]
        rest = share_ref.shape[1] - split
        share_ref[first : first + 16, split:] = right[first : first + 16, :rest]


def call(kernel, shapes, operands, extra=()):
    size = operands[1].shape[-1] if extra else 0
    scratch = []
    for rows in extra:
        held = pltpu.VMEM((size + rows, size), jnp.float32)
        scratch += [held, held, pltpu.VMEM((BLOCK, BLOCK), jnp.float32)]
    return pl.pallas_call(
        kernel,
        out_shape=[jax.ShapeDtypeStruct(shape, jnp.float32) for shape in shapes],
        in_specs=[pl.BlockSpec(memory_space=pltpu.VMEM)] * len(operands),
        out_specs=[
            pl.BlockSpec(memory_space=pltpu.SMEM if shape == (1, 1) else pltpu.VMEM)
            for shape in shapes
        ],
        scratch_shapes=scratch,
        compiler_params=pltpu.CompilerParams(vmem_limit_bytes=40 * 2**20),
        cost_estimate=pl.CostEstimate(
            flops=1024 * math.prod(shapes[0]) + 2 * size**3,
            bytes_accessed=8 * math.prod(shapes[0]),
            transcendentals=size,
        ),
    )(*operands)


def gather(piece, axes):
    copies = jnp.broadcast_to(piece[None], (lax.axis_size(axes),) + piece.shape)
    return lax.all_to_all(copies, axes, 0, 0, tiled=True)


def gram_rows(left, right):
    return lax.dot_general(
        left,
        right,
        (((0,), (0,)), ((), ())),
        precision=HIGHEST,
        preferred_element_type=jnp.float32,
    )


def exchange_halves(partial_image):
    return jnp.sum(lax.all_to_all(partial_image, "core", 0, 0, tiled=True), axis=0)


def gather_gram(piece):
    size = piece.size
    eight = gather(piece, ("y", "col")).reshape(-1, size)
    four = gather(eight, ("x",)).reshape(-1, size)
    return gather(four, ("core",)).reshape(size, size)


def by_basis(grams, sketch, turned, scales):
    size, image_rows = sketch.shape[1], 16
    (partial_image,) = call(
        left_kernel,
        [(2, turned.shape[0] // 2, size)],
        [grams, sketch, turned],
        (sketch.shape[0],),
    )
    parts = exchange_halves(partial_image).astype(jnp.bfloat16).reshape(-1, image_rows, size)
    parts = lax.all_to_all(parts, ("y", "x"), 0, 0, tiled=True)
    image = jnp.sum(parts.astype(jnp.float32), axis=0)

    near = gather(image, ("x", "core")).reshape(-1, size)
    start = (lax.axis_index("core") * 4 + lax.axis_index("x")) * (size // 8)
    chosen = lax.dynamic_slice_in_dim(near, start, size // 8, 1)
    share = gram_rows(chosen, near).reshape(size // 8, 4, size // 4)
    share = lax.all_to_all(share, ("y", "col"), 0, 0, tiled=True)
    gram_right = gather_gram(jnp.sum(share, axis=0))
    q_right, triangle = call(
        functools.partial(right_kernel, scales),
        [(image_rows, size), (size, size)],
        [gram_right, image],
        (image_rows,),
    )
    return (q_right, triangle)


def per_device(hidden_states, sketch_matrix):
    rows, block_width = hidden_states.shape
    size = sketch_matrix.shape[1]
    cols, spread = lax.axis_size("col"), lax.axis_size(ROW)
    own_rows, image_rows = rows // cols, block_width // spread
    root_rows, root_width = math.sqrt(rows * spread), math.sqrt(block_width * cols)
    turned = hidden_states.T

    def halved(packed, axes):
        packed = packed.astype(jnp.float16)
        return lax.all_to_all(packed, axes, 0, 0, tiled=True).astype(jnp.float32)

    many, few = TILES * own_rows + 8, TILES * image_rows + 8
    packed = pl.pallas_call(
        sketch_kernel,
        out_shape=jax.ShapeDtypeStruct((cols, many, LANES), jnp.float32),
        in_specs=[pl.BlockSpec(memory_space=pl.ANY)] * 2,
        out_specs=pl.BlockSpec(memory_space=pltpu.VMEM),
        scratch_shapes=[
            pltpu.VMEM(hidden_states.shape, jnp.bfloat16),
            pltpu.VMEM(sketch_matrix.shape, jnp.bfloat16),
            pltpu.SemaphoreType.DMA((4, 2)),
        ],
        compiler_params=pltpu.CompilerParams(vmem_limit_bytes=40 * 2**20),
    )(hidden_states, sketch_matrix)
    (packed,) = call(own_kernel, [(cols, many, LANES)], [halved(packed, "col")])
    parts = halved(packed, "col")

    half = block_width // 2
    partial_raw, sketch = call(raw_kernel, [(2, half, size), (rows, size)], [turned, parts])
    column = lax.axis_index("col")
    own = lax.dynamic_slice_in_dim(sketch, column * own_rows, own_rows, 0)
    halves = lax.all_to_all(partial_raw, "core", 0, 0, tiled=True)
    (packed,) = call(halves_kernel, [(spread // 2, few, LANES)], [halves])
    (packed,) = call(own_kernel, [(cols, few, LANES)], [halved(packed, ("y", "x"))])
    parts = halved(packed, "col")

    wide = size + BLOCK
    col = jnp.full((8, 128), column, jnp.int32)
    (left,) = call(left_share_kernel, [(spread, size)], [col, sketch])
    share, near = call(share_kernel, [(spread, wide), (cols * image_rows, size)], [col, left, parts])
    raw = lax.dynamic_slice_in_dim(near, column * image_rows, image_rows, 0)
    share = lax.all_to_all(share.reshape(spread, 1, wide), ROW, 0, 0, tiled=True)
    eight = gather(jnp.sum(share, axis=0), ("y", "col")).reshape(spread, wide)
    grams = gather(gather(eight, ("x",)), ("core",))

    scales = (root_rows, root_width, 1.0 / root_width)
    q_left, q_right, triangle, margin = call(
        functools.partial(both_kernel, scales),
        [(own_rows, size), (image_rows, size), (size, size), (1, 1)],
        [grams, own, raw],
        (own_rows + size, image_rows),
    )
    q_right, triangle = lax.cond(
        margin[0, 0] > ENOUGH,
        lambda: (q_right, triangle),
        lambda: by_basis(grams, sketch, turned, scales[1:]),
    )
    return (q_left, q_right.reshape(1, image_rows, size), triangle)


def solution(mesh):
    fine = Mesh(mesh.devices.reshape(8, 4, 2, 8), ROW + ("col",))
    return jax.shard_map(
        per_device,
        mesh=fine,
        in_specs=(P(ROW, "col"), P("col", None)),
        out_specs=(P(ROW + ("col",), None), P("col", ROW, None), P()),
        check_vma=False,
    )
```
